32 devices in a mesh: groups: 2 (over x), team: 2 (over core), blk: 8 (over z, y).
Axes of the slice: x: 2, y: 2, z: 4, core: 2. Of those that a mesh axis runs over, the one named last changes fastest.
Arguments:
- probe: bfloat16 [192, 32, 128], P(('groups', 'blk')), parts along dimension 0, may hold values from -6 to 6
- positions: float32 [192, 3, 128], P(('groups', 'blk')), parts along dimension 0, as said below
- conductivity: float32 [192, 128], P(('groups', 'blk')), parts along dimension 0, may hold values from 0.5 to 2
- fluid_exchange: float32 [192, 128], P(('groups', 'blk')), parts along dimension 0, may hold values from 0.5 to 8
- row_blocks: int32 [192], P(('groups', 'blk')), parts along dimension 0, may hold values from 1 to 27, 864 in all
- column_blocks: int32 [192, 27], P(('groups', 'blk')), parts along dimension 0, may hold values from 0 to 95, as said below
Outputs:
- filtered: float32 [192, 32, 128], P(('groups', 'blk')), parts along dimension 0
The draws below stay inside these ranges and needn't reach their ends.
There are 2 independent parts, one for each index of `groups`. The reference program is written for one: setup_inputs(seed, part) draws one part's arguments, and reference() takes and returns one part's arrays. A program takes and returns all parts, laid end to end along the dimension named above; each array names one. Nothing has to cross between parts.
Inputs may be any that keep to these rules, and one draw needn't show every extreme that they name: `row_blocks`: every row lists at least one block; the counts of one bed sum to 864. `column_blocks`: ids in slots at or beyond a row's count are ignored; ids may repeat within a row. Every id differs from its row I by at most 24 around the closed order of the 96 clusters (J = (I + d) mod 96, |d| <= 24), and both ends of that reach occur. `positions`: clusters close in index lie close in space.
All inputs are finite; a program needn't handle non-finite values.
Results may differ from the reference program's by a relative error of at most 0.0029.
Values may be sent and summed in bfloat16 or wider, within the bound.
A program may use at most 64 MiB of HBM per device.

```python
import math
import jax
import jax.numpy as jnp
import numpy as np
from jax import lax

CL = 128
PROBE = 32
CT = 12
MAXB = 27
MEANB = 9
DEGREE = 8
NC = 96


def draw_column_blocks(key, part):
    reach = 2 * CT
    offsets = jax.random.randint(jax.random.fold_in(key, 11), (NC, MAXB), -reach, reach + 1)
    first_row = jax.random.randint(jax.random.fold_in(key, 12), (), 0, NC)
    second_row = (first_row + 1) % NC
    rows = jnp.arange(NC, dtype=jnp.int32)
    slot_zero = (jnp.arange(MAXB, dtype=jnp.int32) == 0)[None, :]
    offsets = jnp.where((rows == first_row)[:, None] & slot_zero, reach, offsets)
    offsets = jnp.where((rows == second_row)[:, None] & slot_zero, -reach, offsets)
    return ((rows[:, None] + offsets) % NC).astype(jnp.int32)


def draw_positions(key, part):
    spread = jnp.clip(jax.random.normal(jax.random.fold_in(key, 21), (NC, 3, CL), jnp.float32), -6.0, 6.0)
    radius = 0.6 / (2.0 * math.sin(math.pi * 2.0 * CT / NC))
    angle = 2.0 * math.pi * jnp.arange(NC, dtype=jnp.float32) / NC
    centre = jnp.stack([radius * jnp.cos(angle), radius * jnp.sin(angle), jnp.zeros((NC,), jnp.float32)], axis=1)
    return (spread + centre[:, :, None]).astype(jnp.float32)


def level_of(stream_key, extent, shards, smallest, high):
    gain, own = 1.0, jax.random.fold_in(stream_key, 6)
    for axis_at, parts in shards:
        steps = jnp.exp(jax.random.uniform(jax.random.fold_in(own, axis_at), (parts,), jnp.float32, smallest / len(shards), high / len(shards)))
        gain = gain * jnp.repeat(steps, extent[axis_at] // parts).reshape([-1 if axis == axis_at else 1 for axis in range(len(extent))])
    return gain


def profile(number_of, total, most, lean):
    loads = [(1 << 20) // math.isqrt(standing ** lean) + 1 for standing in range(2, number_of + 1)]
    rest, counts = total - most - (number_of - 1), [1] * (number_of - 1)
    while rest > 0:
        free = [i for i in range(number_of - 1) if counts[i] < most]
        whole, budget = sum([loads[i] for i in free]), rest
        for i in free:
            addition = min(most - counts[i], max(1, budget * loads[i] // whole), rest)
            counts[i] = counts[i] + addition
            rest = rest - addition
    return np.array([most] + counts)


def ragged_sizes(own_key, amount, total, bound, lean):
    if amount == 2:
        one = jax.random.randint(own_key, (), max(1, total - bound), min(bound, total - 1) + 1)
        return jnp.stack([one, total - one])
    tallies = jnp.asarray(profile(amount, total, bound, lean), jnp.int32)
    twos = (amount - 1) // 2
    source_of, taker = tallies[1:1 + 2 * twos:2], tallies[2:2 + 2 * twos:2]
    room = jnp.minimum(source_of - 1, bound - taker)
    shifted = jax.random.randint(jax.random.fold_in(own_key, 1), (twos,), 0, 1 << 20) % (room + 1)
    tallies = tallies.at[1:1 + 2 * twos:2].set(source_of - shifted).at[2:2 + 2 * twos:2].set(taker + shifted)
    return tallies[jax.random.permutation(jax.random.fold_in(own_key, 2), amount)]


def centred(key, dims, scale, most, shards=(), kind=jnp.bfloat16):
    loudness = level_of(key, dims, shards, -0.22, 0.18) if shards else 1.0
    entries = jax.random.normal(key, dims, jnp.float32) * scale * loudness
    return jnp.minimum(jnp.maximum(entries, -most), most).astype(kind)


def setup_inputs(seed: int = 0, part: int = 0) -> dict:
    key_of = jax.random.split(jax.random.key(seed), 7)
    part_splits = jax.random.split(jax.random.fold_in(key_of[6], part), 7)
    probe = centred(part_splits[0], (NC, PROBE, CL), 1.0, 6.0, ((0, 8),))
    positions = draw_positions(jax.random.fold_in(jax.random.fold_in(key_of[6], part), 71), part)
    conductivity = jnp.clip(jnp.exp(math.log(2.0) - 1.3862944 * jax.random.uniform(part_splits[2], (NC, CL), jnp.float32) ** level_of(part_splits[2], (NC, CL), ((0, 8),), -0.2, 0.2)), 0.5, 2.0)
    fluid_exchange = jnp.clip(jnp.exp(math.log(8.0) - 2.7725887 * jax.random.uniform(part_splits[3], (NC, CL), jnp.float32) ** level_of(part_splits[3], (NC, CL), ((0, 8),), -0.2, 0.2)), 0.5, 8.0)
    row_blocks = ragged_sizes(part_splits[4], NC, MEANB * NC, MAXB, 2).astype(jnp.int32)
    column_blocks = draw_column_blocks(jax.random.fold_in(jax.random.fold_in(key_of[6], part), 71), part)
    return dict(probe=probe, positions=positions, conductivity=conductivity, fluid_exchange=fluid_exchange, row_blocks=row_blocks, column_blocks=column_blocks)


WIDTH_SQ = 0.245
CENTER = 1.05
HALF_SPAN = 0.95


def conductance(row_pos, row_kappa, col_pos, col_kappa):
    offset = row_pos[..., :, :, None] - col_pos[..., :, None, :]
    dist_sq = jnp.sum(offset * offset, axis=-3)
    left = row_kappa[..., :, None]
    right = col_kappa[..., None, :]
    return 2.0 * left * right / (left + right) * jnp.exp(-dist_sq / WIDTH_SQ)


def apply_rows(probe_values, positions, conductivity, row_blocks, column_blocks):
    slot_ids = jnp.arange(MAXB, dtype=jnp.int32)
    diagonal_mask = jnp.eye(CL, dtype=bool)

    def row_terms(row_index):
        col_ids = column_blocks[row_index]
        conduct = conductance(positions[row_index][None], conductivity[row_index][None], positions[col_ids], conductivity[col_ids])
        active = (slot_ids < row_blocks[row_index])[:, None, None]
        itself = (col_ids == row_index)[:, None, None] & diagonal_mask[None]
        conduct = jnp.where(active & jnp.logical_not(itself), conduct, jnp.float32(0.0))
        degree = jnp.sum(conduct, axis=(0, 2))
        rounded = lax.optimization_barrier(conduct.astype(jnp.bfloat16))
        tile_values = rounded.astype(jnp.float32)
        gathered = probe_values[col_ids].astype(jnp.float32)
        product = jnp.einsum("sij,smj->mi", tile_values, gathered)
        return product, degree

    return lax.map(row_terms, jnp.arange(NC, dtype=jnp.int32))


def reference(probe, positions, conductivity, fluid_exchange, row_blocks, column_blocks):
    def operate(current):
        probe_values = current.astype(jnp.bfloat16)
        product, degree = apply_rows(probe_values, positions, conductivity, row_blocks, column_blocks)
        return current - product / (fluid_exchange + degree)[:, None, :]

    previous = probe.astype(jnp.float32)
    current = (operate(previous) - CENTER * previous) / HALF_SPAN
    for iteration in range(DEGREE - 1):
        following = 2.0 * (operate(current) - CENTER * current) / HALF_SPAN - previous
        previous, current = current, following
    return current
```

```python
import functools
import math

import jax
import jax.numpy as jnp
from jax import lax
from jax.experimental import pallas as pl
from jax.experimental.pallas import tpu as pltpu
from jax.sharding import PartitionSpec as P

DEGREE = 8
WIDTH_SQ = 0.245
CENTER = 1.05
HALF_SPAN = 0.95
SCALE = math.sqrt(math.log2(math.e) / WIDTH_SQ)
MESH = pl.DeviceIdType.MESH
REACHES = (-2, -1, 1, 2)
CHUNK = 3
MEAN_BLOCKS = 9
APPROX = True
UNROLL = 54


def kernel(
    teams, probe_in, pos_in, cond_in, fluid_in, counts_in, cols_in, out,
    probe, pos, cond, fluid, counts, cols, load_sem,
    geo, bcast, tiles, even, odd, cur, prev, inv, corr, ids, other,
    geo_send, geo_recv, win_send, win_recv, pair_send, pair_recv,
):
    loads = [
        pltpu.make_async_copy(source, place, load_sem.at[n])
        for n, (source, place) in enumerate(
            (
                (pos_in, pos), (cond_in, cond), (probe_in, probe),
                (cols_in, cols), (counts_in, counts), (fluid_in, fluid),
            )
        )
    ]
    for load in loads:
        load.start()
    rows, columns, particles = probe.shape
    half = columns // 2
    slots = cols.shape[1]
    clusters = teams * rows
    group = lax.axis_index("groups")
    member = lax.axis_index("team")
    team = lax.axis_index("blk")

    def at(reach):
        return (group, member, lax.rem(team + reach + teams, teams))

    partner = (group, 1 - member, team)
    barrier = pltpu.get_barrier_semaphore()
    for reach in REACHES:
        pl.semaphore_signal(barrier, inc=1, device_id=at(reach), device_id_type=MESH)
    pl.semaphore_signal(barrier, inc=1, device_id=partner, device_id_type=MESH)

    for load in loads[:3]:
        load.wait()
    for r in range(rows):
        geo[2, r, 0:3, :] = pos[r] * SCALE
        geo[2, r, 3:4, :] = 0.5 / cond[r : r + 1, :]
        mine = probe[r, pl.ds(pl.multiple_of(member * half, half), half), :]
        even[2 * rows + r] = mine
        cur[r] = mine.astype(jnp.float32)
        prev[r] = jnp.zeros((half, particles), jnp.float32)
    pl.semaphore_wait(barrier, len(REACHES) + 1)

    def geo_copy(n):
        reach = REACHES[n]
        return pltpu.make_async_remote_copy(
            src_ref=geo.at[2], dst_ref=geo.at[2 - reach],
            send_sem=geo_send.at[n], recv_sem=geo_recv.at[n],
            device_id=at(reach), device_id_type=MESH,
        )

    def win_copy(parity, n, first=0, size=None):
        reach = REACHES[n]
        window = (even, odd)[parity]
        size = rows if size is None else size
        return pltpu.make_async_remote_copy(
            src_ref=window.at[pl.ds(2 * rows + first, size)], dst_ref=window.at[pl.ds((2 - reach) * rows + first, size)],
            send_sem=win_send.at[parity, n], recv_sem=win_recv.at[parity, n],
            device_id=at(reach), device_id_type=MESH,
        )

    for n in range(4):
        geo_copy(n).start()
    def spread(place):
        def one(r, carry):
            for k in range(4):
                line = geo[place, r, k : k + 1, :]
                bcast[place * rows + r, k] = jnp.broadcast_to(line, (particles, particles)).T
            return carry
        lax.fori_loop(0, rows, one, 0, unroll=2)

    spread(2)
    for n in range(4):
        geo_copy(n).wait()
        spread(2 - REACHES[n])
    for n in range(4):
        win_copy(0, n).start()

    for load in loads[3:]:
        load.wait()
    base = (team - 2) * rows

    def build_row(r, carry):
        own = team * rows + r
        count = counts[r]
        xi = [jnp.broadcast_to(geo[2, r, k : k + 1, :], (8, particles)) for k in range(4)]

        def build_tile(s, state):
            total, selves = state
            col = cols[r, s]
            active = s < count
            place = col - base
            place = jnp.where(place < 0, place + clusters, place)
            place = jnp.where(place >= clusters, place - clusters, place)
            place = jnp.where(active, jnp.minimum(place, 5 * rows - 1), 0)
            ids[r, s] = place
            selves = selves + jnp.where(active & (col == own), 1.0, 0.0)
            bias = jnp.where(active, 0.0, -1e30)
            for j in range(0, particles, 16):
                parts = []
                for h in (j, j + 8):
                    dx = bcast[place, 0, h : h + 8, :] - xi[0]
                    dy = bcast[place, 1, h : h + 8, :] - xi[1]
                    dz = bcast[place, 2, h : h + 8, :] - xi[2]
                    power = bias - dx * dx - dy * dy - dz * dz
                    value = jnp.exp2(power) / (bcast[place, 3, h : h + 8, :] + xi[3])
                    total = total + value
                    parts.append(value)
                tiles[r, pl.ds(pl.multiple_of(s * particles + j, 16), 16), :] = jnp.concatenate(
                    parts, 0
                ).astype(jnp.bfloat16)
            return total, selves

        total, selves = lax.fori_loop(
            0, slots, build_tile, (jnp.zeros((8, particles), jnp.float32), jnp.float32(0.0)),
            unroll=3,
        )
        itself = 1.0 / (xi[3] + xi[3])
        degree = jnp.sum(total, axis=0, keepdims=True) - selves * itself[0:1]
        divisor = fluid[pl.ds(r, 1), :] + degree
        inv[r] = jnp.broadcast_to((2.0 / HALF_SPAN) / divisor, (half, particles))
        rounded = itself[0:1].astype(jnp.bfloat16).astype(jnp.float32)
        corr[r] = jnp.broadcast_to(selves * rounded, (half, particles))
        return carry

    lax.fori_loop(0, rows, build_row, 0)

    def step(k, now):
        later = 1 - now
        window, target = (even, odd)[now], (even, odd)[later]
        for n in range(4):
            win_copy(now, n).wait()
        gain = jnp.where(k == 0, 0.5, 1.0)

        def row(r):
            taken = jnp.concatenate(
                [window[ids[r, s]] for s in range(slots)],
                axis=1,
            )
            product = jnp.dot(taken, tiles[r], preferred_element_type=jnp.float32)
            mine = window[2 * rows + r].astype(jnp.float32)
            product = product - corr[r] * mine
            field = cur[r]
            change = (2.0 * (1.0 - CENTER) / HALF_SPAN) * field - product * inv[r]
            fresh = gain * change - prev[r]
            prev[r] = field
            cur[r] = fresh
            target[2 * rows + r] = fresh.astype(jnp.bfloat16)

        for first in range(0, rows, CHUNK):
            size = min(CHUNK, rows - first)
            for r in range(first, first + size):
                row(r)

            @pl.when(k < DEGREE - 1)
            def _():
                for n in range(4):
                    win_copy(later, n, first, size).start()

    def two_steps(i, carry):
        step(2 * i, 0)
        step(2 * i + 1, 1)
        return carry

    lax.fori_loop(0, DEGREE // 2, two_steps, 0)

    swap = pltpu.make_async_remote_copy(
        src_ref=cur, dst_ref=other, send_sem=pair_send, recv_sem=pair_recv,
        device_id=partner, device_id_type=MESH,
    )
    swap.start()
    out[:, pl.ds(pl.multiple_of(member * half, half), half), :] = cur[...]
    swap.wait()
    out[:, pl.ds(pl.multiple_of((1 - member) * half, half), half), :] = other[...]


def local(teams, probe, positions, conductivity, fluid_exchange, row_blocks, column_blocks):
    rows, columns, particles = probe.shape
    slots = column_blocks.shape[1]
    half = columns // 2
    vmem = pl.BlockSpec(memory_space=pltpu.VMEM)
    anywhere = pl.BlockSpec(memory_space=pl.ANY)
    f32 = jnp.float32
    return pl.pallas_call(
        functools.partial(kernel, teams),
        out_shape=jax.ShapeDtypeStruct((rows, columns, particles), f32),
        in_specs=[anywhere] * 6,
        out_specs=vmem,
        scratch_shapes=[
            pltpu.VMEM(probe.shape, probe.dtype),
            pltpu.VMEM(positions.shape, f32),
            pltpu.VMEM(conductivity.shape, f32),
            pltpu.VMEM(fluid_exchange.shape, f32),
            pltpu.SMEM(row_blocks.shape, jnp.int32),
            pltpu.SMEM(column_blocks.shape, jnp.int32),
            pltpu.SemaphoreType.DMA((6,)),
            pltpu.VMEM((5, rows, 4, particles), f32),
            pltpu.VMEM((5 * rows, 4, particles, particles), f32),
            pltpu.VMEM((rows, slots * particles, particles), jnp.bfloat16),
            pltpu.VMEM((5 * rows, half, particles), jnp.bfloat16),
            pltpu.VMEM((5 * rows, half, particles), jnp.bfloat16),
            pltpu.VMEM((rows, half, particles), f32),
            pltpu.VMEM((rows, half, particles), f32),
            pltpu.VMEM((rows, half, particles), f32),
            pltpu.VMEM((rows, half, particles), f32),
            pltpu.SMEM((rows, slots), jnp.int32),
            pltpu.VMEM((rows, half, particles), f32),
            pltpu.SemaphoreType.DMA((4,)),
            pltpu.SemaphoreType.DMA((4,)),
            pltpu.SemaphoreType.DMA((2, 4)),
            pltpu.SemaphoreType.DMA((2, 4)),
            pltpu.SemaphoreType.DMA,
            pltpu.SemaphoreType.DMA,
        ],
        compiler_params=pltpu.CompilerParams(
            collective_id=0, has_side_effects=True, vmem_limit_bytes=60 * 1024 * 1024
        ),
    )(probe, positions, conductivity, fluid_exchange, row_blocks, column_blocks)


def bed_kernel(
    teams, total, probe_in, pos_in, cond_in, fluid_in, counts_in, cols_in, out,
    probe, pos, cond, load_sem,
    geo, ints, cnts, counts, cols, smem_sem, fluid, stage, landed,
    bcast, tiles, ends, begins, ids, keep, selfs, more, last,
    sums, parts, low, high, cur, prev, inv, corr, mine_sum, their_sum, mine_deg, their_deg, arrived,
    gather_send, gather_recv, pair_send, pair_recv,
):
    rows, columns, particles = probe.shape
    slots = cols.shape[1]
    clusters = teams * rows
    width = columns // teams
    pairs = clusters // 2
    units = tiles.shape[0]
    span = 2 * units
    group = lax.axis_index("groups")
    member = lax.axis_index("team")
    team = lax.axis_index("blk")
    f32, bf16 = jnp.float32, jnp.bfloat16

    def at(ahead):
        return (group, member, lax.rem(team + ahead, teams))

    partner = (group, 1 - member, team)
    barrier = pltpu.get_barrier_semaphore()
    for ahead in range(1, teams):
        pl.semaphore_signal(barrier, inc=1, device_id=at(ahead), device_id_type=MESH)
    pl.semaphore_signal(barrier, inc=1, device_id=partner, device_id_type=MESH)

    loads = [
        pltpu.make_async_copy(source, place, load_sem.at[n])
        for n, (source, place) in enumerate(
            (
                (pos_in, pos), (cond_in, cond), (probe_in, probe),
                (cols_in, ints.at[team]), (counts_in, cnts.at[team]), (fluid_in, fluid.at[team]),
            )
        )
    ]
    for load in loads:
        load.start()
    for load in loads[:2]:
        load.wait()
    for r in range(rows):
        geo[team, r, 0:3, :] = pos[r] * SCALE
        geo[team, r, 3:4, :] = 0.5 / cond[r : r + 1, :]
    pl.semaphore_wait(barrier, teams)

    def gather(kind, ahead):
        source, place = (
            (counts_in, cnts.at[team]), (cols_in, ints.at[team]), (geo.at[team], geo.at[team]),
            (stage.at[lax.rem(team + ahead, teams)], landed.at[team]), (fluid_in, fluid.at[team]),
        )[kind]
        return pltpu.make_async_remote_copy(
            src_ref=source, dst_ref=place,
            send_sem=gather_send.at[kind, ahead], recv_sem=gather_recv.at[kind, ahead],
            device_id=at(ahead), device_id_type=MESH,
        )

    others = range(1, teams)
    for load in loads[3:5]:
        load.wait()
    for ahead in others:
        gather(2, ahead).start()
    for ahead in others:
        gather(0, ahead).start()
        gather(1, ahead).start()

    def spread(place):
        def one(r, carry):
            for k in range(4):
                line = geo[place, r, k : k + 1, :]
                bcast[place * rows + r, k] = jnp.broadcast_to(line, (particles, particles)).T
            return carry
        lax.fori_loop(0, rows, one, 0, unroll=4)

    spread(team)
    loads[2].wait()
    loads[5].wait()
    for q in range(rows // 4):
        wide = [probe[4 * q + a].astype(f32) for a in range(4)]
        for t in range(teams):
            stage[t, q] = jnp.concatenate([w[t * width : (t + 1) * width] for w in wide], 0).astype(bf16)
    landed[team] = stage[team]
    for ahead in others:
        gather(0, ahead).wait()
        gather(1, ahead).wait()
    moves = [
        pltpu.make_async_copy(cnts, counts, smem_sem.at[teams]),
    ] + [
        pltpu.make_async_copy(ints.at[t], cols.at[pl.ds(t * rows, rows)], smem_sem.at[t]) for t in range(teams)
    ]
    for move in moves:
        move.start()
    for ahead in others:
        gather(2, ahead).wait()
        spread(lax.rem(team + teams - ahead, teams))
    for ahead in others:
        gather(3, ahead).start()
        gather(4, ahead).start()
    for move in moves:
        move.wait()

    first = member * span
    final = first + span

    def lay(t, state):
        at_end, zero, one = state
        for j in range(rows):
            r = t * rows + j
            begins[r] = at_end
            at_end = at_end + counts[t, 0, j]
            ends[r] = at_end
            zero = zero + jnp.where(at_end <= first, 1, 0)
            one = one + jnp.where(at_end <= first + units, 1, 0)
        return at_end, zero, one

    _, zero, one = lax.fori_loop(0, teams, lay, (jnp.int32(0), jnp.int32(0), jnp.int32(0)))
    zero, one = jnp.minimum(zero, clusters - 1), jnp.minimum(one, clusters - 1)

    def build_tile(u, lane, r, selves, running):
        place = first + lane * units + u
        index = lane * units + u
        r = jnp.minimum(r + jnp.where(place >= ends[r], 1, 0), clusters - 1)
        begin = begins[r]
        col = cols[r, jnp.minimum(place - begin, slots - 1)]
        fresh = jnp.logical_or(place == begin, u == 0)
        going = jnp.where(fresh, 0.0, 1.0)
        ids[index] = col
        keep[index] = going
        selves = jnp.where(fresh, 0.0, selves) + jnp.where(col == r, 1.0, 0.0)
        selfs[index] = selves
        t = lax.div(r, rows)
        xi = [jnp.broadcast_to(geo[t, r - t * rows, k : k + 1, :], (8, particles)) for k in range(4)]
        tally = jnp.zeros((8, particles), f32)
        for j in range(0, particles, 16):
            values = []
            for h in (j, j + 8):
                dx = bcast[col, 0, h : h + 8, :] - xi[0]
                dy = bcast[col, 1, h : h + 8, :] - xi[1]
                dz = bcast[col, 2, h : h + 8, :] - xi[2]
                power = dx * dx + dy * dy + dz * dz
                value = pltpu.reciprocal((bcast[col, 3, h : h + 8, :] + xi[3]) * jnp.exp2(power), approx=APPROX)
                tally = tally + value
                values.append(value)
            tiles[u, lane * particles + j : lane * particles + j + 16, :] = jnp.concatenate(values, 0).astype(bf16)
        running = running * going + tally
        sums[index] = running
        return r, selves, running

    def build(u, state):
        return build_tile(u, 0, *state[:3]) + build_tile(u, 1, *state[3:])

    blank = jnp.zeros((8, particles), f32)
    state = lax.fori_loop(
        0, units, build, (zero, jnp.float32(0.0), blank, one, jnp.float32(0.0), blank), unroll=2
    )

    sums[span] = blank
    parts[span] = blank
    edge_row = state[0]
    edge = ends[edge_row]
    for u in range(slots - 1):
        flag = jnp.where(first + units + u < edge, 1.0, 0.0)
        more[u] = flag
        selfs[units + u] = selfs[units + u] + flag * selfs[units - 1]
        sums[units + u] = sums[units + u] + flag * sums[units - 1]
    half = lax.broadcasted_iota(jnp.int32, (8, particles), 0) < width

    def both(even, odd):
        return jnp.where(half, jnp.broadcast_to(even, (8, particles)), jnp.broadcast_to(odd, (8, particles)))

    def settle(t, carry):
        for j in range(0, rows, 2):
            r = t * rows + j
            p = t * (rows // 2) + j // 2
            lines = []
            for h in (0, 1):
                end = jnp.minimum(ends[r + h], final) - 1
                have = end >= jnp.maximum(begins[r + h], first)
                spot = jnp.where(have, end - first, span)
                last[r + h] = spot
                own = jnp.where(have, selfs[jnp.where(have, end - first, 0)], 0.0)
                twice = geo[t, j + h, 3:4, :] + geo[t, j + h, 3:4, :]
                itself = pltpu.reciprocal(twice, approx=APPROX)
                degree = jnp.sum(sums[spot], axis=0, keepdims=True) - own * itself
                lines.append((degree, own * itself.astype(bf16).astype(f32)))
            mine_deg[p] = both(lines[0][0], lines[1][0])
            corr[p] = both(lines[0][1], lines[1][1])
        return carry

    lax.fori_loop(0, teams, settle, 0)

    def swap(source, place, n):
        return pltpu.make_async_remote_copy(
            src_ref=source, dst_ref=place, send_sem=pair_send.at[n], recv_sem=pair_recv.at[n],
            device_id=partner, device_id_type=MESH,
        )

    degrees = swap(mine_deg, their_deg, 2)
    degrees.start()

    nothing = jnp.zeros((8, particles), f32)

    def publish(p, fresh):
        turned = pltpu.roll(fresh, width, 0)
        for h, line in ((0, jnp.where(half, fresh, turned)), (1, jnp.where(half, turned, fresh))):
            low[2 * p + h] = jnp.concatenate([line, nothing], 0).astype(bf16)
            high[2 * p + h] = jnp.concatenate([nothing, line], 0).astype(bf16)

    for ahead in others:
        gather(3, ahead).wait()
        gather(4, ahead).wait()

    def begin_fields(t, carry):
        for q in range(rows // 4):
            block = landed[t, q].astype(f32)
            for h in (0, 1):
                p = t * (rows // 2) + 2 * q + h
                cur[p] = block[8 * h : 8 * h + 8]
                prev[p] = nothing
                publish(p, block[8 * h : 8 * h + 8])
        return carry

    lax.fori_loop(0, teams, begin_fields, 0)

    degrees.wait()

    def divide(t, carry):
        for j in range(0, rows, 2):
            p = t * (rows // 2) + j // 2
            exchange = both(fluid[t, j : j + 1, :], fluid[t, j + 1 : j + 2, :])
            inv[p] = (2.0 / HALF_SPAN) / (exchange + (mine_deg[p] + their_deg[p]))
        return carry

    lax.fori_loop(0, teams, divide, 0)

    def step(k, carry):
        slot = lax.rem(k, 2)

        def unit(u, state):
            taken = jnp.concatenate([low[ids[u]], high[ids[units + u]]], axis=1)
            product = jnp.dot(taken, tiles[u], preferred_element_type=f32)
            zero = state[0] * keep[u] + product[0:8]
            one = state[1] * keep[units + u] + product[8:16]
            parts[u] = zero
            parts[units + u] = one
            return zero, one

        lax.fori_loop(0, units, unit, (blank, blank), unroll=UNROLL)
        for u in range(slots - 1):
            parts[units + u] = parts[units + u] + more[u] * parts[units - 1]

        def pack(p, carry):
            own = cur[p].astype(bf16).astype(f32)
            product = jnp.where(half, parts[last[2 * p]], parts[last[2 * p + 1]])
            mine_sum[slot, p] = product - corr[p] * own
            return carry

        lax.fori_loop(0, pairs, pack, 0, unroll=8)
        exchange = swap(mine_sum.at[slot], their_sum.at[slot], slot)
        exchange.start()
        exchange.wait()
        gain = jnp.where(k == 0, 0.5, 1.0)

        def update(p, carry):
            field = cur[p]
            product = mine_sum[slot, p] + their_sum[slot, p]
            change = (2.0 * (1.0 - CENTER) / HALF_SPAN) * field - product * inv[p]
            fresh = gain * change - prev[p]
            prev[p] = field
            cur[p] = fresh
            publish(p, fresh)
            return carry

        lax.fori_loop(0, pairs, update, 0, unroll=8)
        return carry

    lax.fori_loop(0, DEGREE, step, 0)

    few = rows // 2

    def deliver(ahead):
        goal = lax.rem(team + ahead, teams)
        return pltpu.make_async_remote_copy(
            src_ref=cur.at[pl.ds(goal * few, few)], dst_ref=arrived.at[team],
            send_sem=gather_send.at[5, ahead], recv_sem=gather_recv.at[5, ahead],
            device_id=at(ahead), device_id_type=MESH,
        )

    for ahead in others:
        deliver(ahead).start()
    for p in range(few):
        arrived[team, p] = cur[team * few + p]
    for ahead in others:
        deliver(ahead).wait()
    for p in range(few):
        for c in range(0, teams, 2):
            one, two = arrived[c, p], arrived[c + 1, p]
            out[2 * p, c * width : c * width + 8, :] = jnp.where(half, one, pltpu.roll(two, width, 0))
            out[2 * p + 1, c * width : c * width + 8, :] = jnp.where(half, pltpu.roll(one, width, 0), two)


def bed(teams, probe, positions, conductivity, fluid_exchange, row_blocks, column_blocks):
    rows, columns, particles = probe.shape
    slots = column_blocks.shape[1]
    clusters = teams * rows
    total = MEAN_BLOCKS * clusters
    units = total // 4
    span = 2 * units
    pairs = clusters // 2
    f32, bf16, i32 = jnp.float32, jnp.bfloat16, jnp.int32
    vmem = pl.BlockSpec(memory_space=pltpu.VMEM)
    anywhere = pl.BlockSpec(memory_space=pl.ANY)
    field = pltpu.VMEM((pairs, 8, particles), f32)
    return pl.pallas_call(
        functools.partial(bed_kernel, teams, total),
        out_shape=jax.ShapeDtypeStruct((rows, columns, particles), f32),
        in_specs=[anywhere] * 6,
        out_specs=vmem,
        scratch_shapes=[
            pltpu.VMEM(probe.shape, probe.dtype),
            pltpu.VMEM(positions.shape, f32),
            pltpu.VMEM(conductivity.shape, f32),
            pltpu.SemaphoreType.DMA((6,)),
            pltpu.VMEM((teams, rows, 4, particles), f32),
            pltpu.VMEM((teams, rows, slots), i32),
            pltpu.VMEM((teams, 1, rows), i32),
            pltpu.SMEM((teams, 1, rows), i32),
            pltpu.SMEM((clusters, slots), i32),
            pltpu.SemaphoreType.DMA((teams + 1,)),
            pltpu.VMEM((teams, rows, particles), f32),
            pltpu.VMEM((teams, rows // 4, 16, particles), bf16),
            pltpu.VMEM((teams, rows // 4, 16, particles), bf16),
            pltpu.VMEM((clusters, 4, particles, particles), f32),
            pltpu.VMEM((units, 2 * particles, particles), bf16),
            pltpu.SMEM((clusters + 1,), i32),
            pltpu.SMEM((clusters + 1,), i32),
            pltpu.SMEM((span,), i32),
            pltpu.SMEM((span,), f32),
            pltpu.SMEM((span,), f32),
            pltpu.SMEM((slots,), f32),
            pltpu.SMEM((clusters,), i32),
            pltpu.VMEM((span + 1, 8, particles), f32),
            pltpu.VMEM((span + 1, 8, particles), f32),
            pltpu.VMEM((clusters, 16, particles), bf16),
            pltpu.VMEM((clusters, 16, particles), bf16),
            field, field, field, field,
            pltpu.VMEM((2, pairs, 8, particles), f32),
            pltpu.VMEM((2, pairs, 8, particles), f32),
            field, field,
            pltpu.VMEM((teams, rows // 2, 8, particles), f32),
            pltpu.SemaphoreType.DMA((6, teams)),
            pltpu.SemaphoreType.DMA((6, teams)),
            pltpu.SemaphoreType.DMA((3,)),
            pltpu.SemaphoreType.DMA((3,)),
        ],
        compiler_params=pltpu.CompilerParams(
            collective_id=1, has_side_effects=True, vmem_limit_bytes=60 * 1024 * 1024
        ),
    )(probe, positions, conductivity, fluid_exchange, row_blocks.reshape(1, rows), column_blocks)


def either(teams, probe, *rest):
    rows, columns, particles = probe.shape
    if columns == 4 * teams and rows % 4 == 0 and MEAN_BLOCKS * teams * rows <= 1024:
        return bed(teams, probe, *rest)
    return local(teams, probe, *rest)


def solution(mesh):
    return jax.shard_map(
        functools.partial(either, mesh.shape["blk"]),
        mesh=mesh,
        in_specs=(
            P(("groups", "blk"), None, None),
            P(("groups", "blk"), None, None),
            P(("groups", "blk"), None),
            P(("groups", "blk"), None),
            P(("groups", "blk")),
            P(("groups", "blk"), None),
        ),
        out_specs=P(("groups", "blk"), None, None),
        check_vma=False,
    )
```

```python
import functools
import math

import jax
import jax.numpy as jnp
from jax import lax
from jax.experimental import pallas as pl
from jax.experimental.pallas import tpu as pltpu
from jax.sharding import PartitionSpec as P

DEGREE = 8
WIDTH_SQ = 0.245
CENTER = 1.05
HALF_SPAN = 0.95
SCALE = math.sqrt(math.log2(math.e) / WIDTH_SQ)
MESH = pl.DeviceIdType.MESH
REACHES = (-2, -1, 1, 2)
CHUNK = 3
MEAN_BLOCKS = 9
APPROX = True
UNROLL = 216
BUILD = 24
SPREAD = 12


def kernel(
    teams, probe_in, pos_in, cond_in, fluid_in, counts_in, cols_in, out,
    probe, pos, cond, fluid, counts, cols, load_sem,
    geo, bcast, tiles, even, odd, cur, prev, inv, corr, ids, other,
    geo_send, geo_recv, win_send, win_recv, pair_send, pair_recv,
):
    loads = [
        pltpu.make_async_copy(source, place, load_sem.at[n])
        for n, (source, place) in enumerate(
            (
                (pos_in, pos), (cond_in, cond), (probe_in, probe),
                (cols_in, cols), (counts_in, counts), (fluid_in, fluid),
            )
        )
    ]
    for load in loads:
        load.start()
    rows, columns, particles = probe.shape
    half = columns // 2
    slots = cols.shape[1]
    clusters = teams * rows
    group = lax.axis_index("groups")
    member = lax.axis_index("team")
    team = lax.axis_index("blk")

    def at(reach):
        return (group, member, lax.rem(team + reach + teams, teams))

    partner = (group, 1 - member, team)
    barrier = pltpu.get_barrier_semaphore()
    for reach in REACHES:
        pl.semaphore_signal(barrier, inc=1, device_id=at(reach), device_id_type=MESH)
    pl.semaphore_signal(barrier, inc=1, device_id=partner, device_id_type=MESH)

    for load in loads[:3]:
        load.wait()
    for r in range(rows):
        geo[2, r, 0:3, :] = pos[r] * SCALE
        geo[2, r, 3:4, :] = 0.5 / cond[r : r + 1, :]
        mine = probe[r, pl.ds(pl.multiple_of(member * half, half), half), :]
        even[2 * rows + r] = mine
        cur[r] = mine.astype(jnp.float32)
        prev[r] = jnp.zeros((half, particles), jnp.float32)
    pl.semaphore_wait(barrier, len(REACHES) + 1)

    def geo_copy(n):
        reach = REACHES[n]
        return pltpu.make_async_remote_copy(
            src_ref=geo.at[2], dst_ref=geo.at[2 - reach],
            send_sem=geo_send.at[n], recv_sem=geo_recv.at[n],
            device_id=at(reach), device_id_type=MESH,
        )

    def win_copy(parity, n, first=0, size=None):
        reach = REACHES[n]
        window = (even, odd)[parity]
        size = rows if size is None else size
        return pltpu.make_async_remote_copy(
            src_ref=window.at[pl.ds(2 * rows + first, size)], dst_ref=window.at[pl.ds((2 - reach) * rows + first, size)],
            send_sem=win_send.at[parity, n], recv_sem=win_recv.at[parity, n],
            device_id=at(reach), device_id_type=MESH,
        )

    for n in range(4):
        geo_copy(n).start()
    def spread(place):
        def one(r, carry):
            for k in range(4):
                line = geo[place, r, k : k + 1, :]
                bcast[place * rows + r, k] = jnp.broadcast_to(line, (particles, particles)).T
            return carry
        lax.fori_loop(0, rows, one, 0, unroll=2)

    spread(2)
    for n in range(4):
        geo_copy(n).wait()
        spread(2 - REACHES[n])
    for n in range(4):
        win_copy(0, n).start()

    for load in loads[3:]:
        load.wait()
    base = (team - 2) * rows

    def build_row(r, carry):
        own = team * rows + r
        count = counts[r]
        xi = [jnp.broadcast_to(geo[2, r, k : k + 1, :], (8, particles)) for k in range(4)]

        def build_tile(s, state):
            total, selves = state
            col = cols[r, s]
            active = s < count
            place = col - base
            place = jnp.where(place < 0, place + clusters, place)
            place = jnp.where(place >= clusters, place - clusters, place)
            place = jnp.where(active, jnp.minimum(place, 5 * rows - 1), 0)
            ids[r, s] = place
            selves = selves + jnp.where(active & (col == own), 1.0, 0.0)
            bias = jnp.where(active, 0.0, -1e30)
            for j in range(0, particles, 16):
                parts = []
                for h in (j, j + 8):
                    dx = bcast[place, 0, h : h + 8, :] - xi[0]
                    dy = bcast[place, 1, h : h + 8, :] - xi[1]
                    dz = bcast[place, 2, h : h + 8, :] - xi[2]
                    power = bias - dx * dx - dy * dy - dz * dz
                    value = jnp.exp2(power) / (bcast[place, 3, h : h + 8, :] + xi[3])
                    total = total + value
                    parts.append(value)
                tiles[r, pl.ds(pl.multiple_of(s * particles + j, 16), 16), :] = jnp.concatenate(
                    parts, 0
                ).astype(jnp.bfloat16)
            return total, selves

        total, selves = lax.fori_loop(
            0, slots, build_tile, (jnp.zeros((8, particles), jnp.float32), jnp.float32(0.0)),
            unroll=3,
        )
        itself = 1.0 / (xi[3] + xi[3])
        degree = jnp.sum(total, axis=0, keepdims=True) - selves * itself[0:1]
        divisor = fluid[pl.ds(r, 1), :] + degree
        inv[r] = jnp.broadcast_to((2.0 / HALF_SPAN) / divisor, (half, particles))
        rounded = itself[0:1].astype(jnp.bfloat16).astype(jnp.float32)
        corr[r] = jnp.broadcast_to(selves * rounded, (half, particles))
        return carry

    lax.fori_loop(0, rows, build_row, 0)

    def step(k, now):
        later = 1 - now
        window, target = (even, odd)[now], (even, odd)[later]
        for n in range(4):
            win_copy(now, n).wait()
        gain = jnp.where(k == 0, 0.5, 1.0)

        def row(r):
            taken = jnp.concatenate(
                [window[ids[r, s]] for s in range(slots)],
                axis=1,
            )
            product = jnp.dot(taken, tiles[r], preferred_element_type=jnp.float32)
            mine = window[2 * rows + r].astype(jnp.float32)
            product = product - corr[r] * mine
            field = cur[r]
            change = (2.0 * (1.0 - CENTER) / HALF_SPAN) * field - product * inv[r]
            fresh = gain * change - prev[r]
            prev[r] = field
            cur[r] = fresh
            target[2 * rows + r] = fresh.astype(jnp.bfloat16)

        for first in range(0, rows, CHUNK):
            size = min(CHUNK, rows - first)
            for r in range(first, first + size):
                row(r)

            @pl.when(k < DEGREE - 1)
            def _():
                for n in range(4):
                    win_copy(later, n, first, size).start()

    def two_steps(i, carry):
        step(2 * i, 0)
        step(2 * i + 1, 1)
        return carry

    lax.fori_loop(0, DEGREE // 2, two_steps, 0)

    swap = pltpu.make_async_remote_copy(
        src_ref=cur, dst_ref=other, send_sem=pair_send, recv_sem=pair_recv,
        device_id=partner, device_id_type=MESH,
    )
    swap.start()
    out[:, pl.ds(pl.multiple_of(member * half, half), half), :] = cur[...]
    swap.wait()
    out[:, pl.ds(pl.multiple_of((1 - member) * half, half), half), :] = other[...]


def local(teams, probe, positions, conductivity, fluid_exchange, row_blocks, column_blocks):
    rows, columns, particles = probe.shape
    slots = column_blocks.shape[1]
    half = columns // 2
    vmem = pl.BlockSpec(memory_space=pltpu.VMEM)
    anywhere = pl.BlockSpec(memory_space=pl.ANY)
    f32 = jnp.float32
    return pl.pallas_call(
        functools.partial(kernel, teams),
        out_shape=jax.ShapeDtypeStruct((rows, columns, particles), f32),
        in_specs=[anywhere] * 6,
        out_specs=vmem,
        scratch_shapes=[
            pltpu.VMEM(probe.shape, probe.dtype),
            pltpu.VMEM(positions.shape, f32),
            pltpu.VMEM(conductivity.shape, f32),
            pltpu.VMEM(fluid_exchange.shape, f32),
            pltpu.SMEM(row_blocks.shape, jnp.int32),
            pltpu.SMEM(column_blocks.shape, jnp.int32),
            pltpu.SemaphoreType.DMA((6,)),
            pltpu.VMEM((5, rows, 4, particles), f32),
            pltpu.VMEM((5 * rows, 4, particles, particles), f32),
            pltpu.VMEM((rows, slots * particles, particles), jnp.bfloat16),
            pltpu.VMEM((5 * rows, half, particles), jnp.bfloat16),
            pltpu.VMEM((5 * rows, half, particles), jnp.bfloat16),
            pltpu.VMEM((rows, half, particles), f32),
            pltpu.VMEM((rows, half, particles), f32),
            pltpu.VMEM((rows, half, particles), f32),
            pltpu.VMEM((rows, half, particles), f32),
            pltpu.SMEM((rows, slots), jnp.int32),
            pltpu.VMEM((rows, half, particles), f32),
            pltpu.SemaphoreType.DMA((4,)),
            pltpu.SemaphoreType.DMA((4,)),
            pltpu.SemaphoreType.DMA((2, 4)),
            pltpu.SemaphoreType.DMA((2, 4)),
            pltpu.SemaphoreType.DMA,
            pltpu.SemaphoreType.DMA,
        ],
        compiler_params=pltpu.CompilerParams(
            collective_id=0, has_side_effects=True, vmem_limit_bytes=60 * 1024 * 1024
        ),
    )(probe, positions, conductivity, fluid_exchange, row_blocks, column_blocks)


def bed_kernel(
    teams, total, probe_in, pos_in, cond_in, fluid_in, counts_in, cols_in, out,
    probe, pos, cond, load_sem,
    geo, ints, cnts, counts, cols, smem_sem, fluid, stage, landed,
    points, mid, lines, flank, tiles, ends, begins, ids, keep, selfs, more, last,
    sums, parts, low, high, cur, prev, inv, corr, mine_sum, their_sum, mine_deg, their_deg, arrived,
    gather_send, gather_recv, pair_send, pair_recv,
):
    rows, columns, particles = probe.shape
    slots = cols.shape[1]
    clusters = teams * rows
    width = columns // teams
    pairs = clusters // 2
    units = tiles.shape[0]
    span = 2 * units
    group = lax.axis_index("groups")
    member = lax.axis_index("team")
    team = lax.axis_index("blk")
    f32, bf16 = jnp.float32, jnp.bfloat16

    def at(ahead):
        return (group, member, lax.rem(team + ahead, teams))

    partner = (group, 1 - member, team)
    barrier = pltpu.get_barrier_semaphore()
    for ahead in range(1, teams):
        pl.semaphore_signal(barrier, inc=1, device_id=at(ahead), device_id_type=MESH)
    pl.semaphore_signal(barrier, inc=1, device_id=partner, device_id_type=MESH)

    loads = [
        pltpu.make_async_copy(source, place, load_sem.at[n])
        for n, (source, place) in enumerate(
            (
                (pos_in, pos), (cond_in, cond), (probe_in, probe),
                (cols_in, ints.at[team]), (counts_in, cnts.at[team]), (fluid_in, fluid.at[team]),
            )
        )
    ]
    for load in loads:
        load.start()
    for load in loads[:2]:
        load.wait()
    for r in range(rows):
        geo[team, r, 0:3, :] = pos[r] * SCALE
        geo[team, r, 3:4, :] = 0.5 / cond[r : r + 1, :]
    pl.semaphore_wait(barrier, teams)

    def gather(kind, ahead):
        source, place = (
            (counts_in, cnts.at[team]), (cols_in, ints.at[team]), (geo.at[team], geo.at[team]),
            (stage.at[lax.rem(team + ahead, teams)], landed.at[team]), (fluid_in, fluid.at[team]),
        )[kind]
        return pltpu.make_async_remote_copy(
            src_ref=source, dst_ref=place,
            send_sem=gather_send.at[kind, ahead], recv_sem=gather_recv.at[kind, ahead],
            device_id=at(ahead), device_id_type=MESH,
        )

    others = range(1, teams)
    for load in loads[3:5]:
        load.wait()
    for ahead in others:
        gather(2, ahead).start()
    for ahead in others:
        gather(0, ahead).start()
        gather(1, ahead).start()

    level = lax.broadcasted_iota(jnp.int32, (8, particles), 0)
    half = level < width
    square = level % width == 3

    def rounded(value):
        return value.astype(bf16).astype(f32)

    def thirds(value):
        head = rounded(value)
        tail = value - head
        body = rounded(tail)
        return head, body, tail - body

    def length(value):
        value = value * value
        value = value + pltpu.roll(value, 1, 0)
        return value + pltpu.roll(value, 2, 0)

    def spread(place):
        def one(r, carry):
            spot = place * rows + r
            point = geo[place, r]
            point = jnp.where(square, 0.0, jnp.concatenate([point, point], 0))
            middle = jnp.broadcast_to(jnp.sum(point * (1.0 / particles), axis=1, keepdims=True), (8, particles))
            points[spot] = point
            mid[spot] = middle
            off = point - middle
            a, b, c = thirds(off)
            d, e, f = thirds(length(off))
            g, h, i = thirds(jnp.broadcast_to(geo[place, r, 3:4, :], (8, particles)))
            last_line = jnp.zeros((8, particles), f32)
            for n, value in enumerate((d, e, f, g, h, i)):
                last_line = jnp.where(level == n, value, last_line)
            block = jnp.concatenate(
                [
                    jnp.where(level == 3, 1.0, jnp.where(half, a, b)),
                    jnp.where(level == 7, 1.0, jnp.where(half, c, a)),
                    jnp.where(level == 7, 1.0, jnp.where(half, b, a)),
                    last_line,
                ],
                0,
            )
            lines[spot] = block.T.astype(bf16)
            flank[spot] = jnp.concatenate(
                [
                    jnp.where(level == 3, g, 0.0),
                    jnp.where(level == 7, h, 0.0),
                    jnp.where(level == 7, i, 0.0),
                    jnp.where((level > 2) & (level < 6), 1.0, 0.0),
                ],
                0,
            ).astype(bf16)
            return carry
        lax.fori_loop(0, rows, one, 0, unroll=SPREAD)

    spread(team)
    loads[2].wait()
    loads[5].wait()
    for q in range(rows // 4):
        wide = [probe[4 * q + a].astype(f32) for a in range(4)]
        for t in range(teams):
            stage[t, q] = jnp.concatenate([w[t * width : (t + 1) * width] for w in wide], 0).astype(bf16)
    landed[team] = stage[team]
    for ahead in others:
        gather(0, ahead).wait()
        gather(1, ahead).wait()
    moves = [
        pltpu.make_async_copy(cnts, counts, smem_sem.at[teams]),
    ] + [
        pltpu.make_async_copy(ints.at[t], cols.at[pl.ds(t * rows, rows)], smem_sem.at[t]) for t in range(teams)
    ]
    for move in moves:
        move.start()
    for ahead in others:
        gather(2, ahead).wait()
        spread(lax.rem(team + teams - ahead, teams))
    for ahead in others:
        gather(3, ahead).start()
        gather(4, ahead).start()
    for move in moves:
        move.wait()

    first = member * span
    final = first + span

    def lay(t, state):
        at_end, zero, one = state
        for j in range(rows):
            r = t * rows + j
            begins[r] = at_end
            at_end = at_end + counts[t, 0, j]
            ends[r] = at_end
            zero = zero + jnp.where(at_end <= first, 1, 0)
            one = one + jnp.where(at_end <= first + units, 1, 0)
        return at_end, zero, one

    _, zero, one = lax.fori_loop(0, teams, lay, (jnp.int32(0), jnp.int32(0), jnp.int32(0)))
    zero, one = jnp.minimum(zero, clusters - 1), jnp.minimum(one, clusters - 1)

    ones = jnp.where(level < 3, 1.0, 0.0)

    def build_tile(u, lane, r, selves, running):
        place = first + lane * units + u
        index = lane * units + u
        r = jnp.minimum(r + jnp.where(place >= ends[r], 1, 0), clusters - 1)
        begin = begins[r]
        col = cols[r, jnp.minimum(place - begin, slots - 1)]
        fresh = jnp.logical_or(place == begin, u == 0)
        going = jnp.where(fresh, 0.0, 1.0)
        ids[index] = col
        keep[index] = going
        selves = jnp.where(fresh, 0.0, selves) + jnp.where(col == r, 1.0, 0.0)
        selfs[index] = selves
        off = points[r] - mid[col]
        a, b, c = thirds(jnp.where(square, length(off), -2.0 * off))
        block = jnp.concatenate([a, jnp.where(half, a, b), jnp.where(half, b, c), ones], 0).astype(bf16)
        both_sides = jnp.dot(
            lines[col], jnp.concatenate([block, flank[r]], 1), preferred_element_type=f32
        )
        tally = jnp.zeros((8, particles), f32)
        for j in range(0, particles, 16):
            values = []
            for h in (j, j + 8):
                power = both_sides[h : h + 8, :particles]
                value = pltpu.reciprocal(both_sides[h : h + 8, particles:] * jnp.exp2(power), approx=APPROX)
                tally = tally + value
                values.append(value)
            tiles[u, lane * particles + j : lane * particles + j + 16, :] = jnp.concatenate(values, 0).astype(bf16)
        running = running * going + tally
        sums[index] = running
        return r, selves, running

    def build(u, state):
        return build_tile(u, 0, *state[:3]) + build_tile(u, 1, *state[3:])

    blank = jnp.zeros((8, particles), f32)
    state = lax.fori_loop(
        0, units, build, (zero, jnp.float32(0.0), blank, one, jnp.float32(0.0), blank), unroll=BUILD
    )

    sums[span] = blank
    parts[span] = blank
    edge_row = state[0]
    edge = ends[edge_row]
    for u in range(slots - 1):
        flag = jnp.where(first + units + u < edge, 1.0, 0.0)
        more[u] = flag
        selfs[units + u] = selfs[units + u] + flag * selfs[units - 1]
        sums[units + u] = sums[units + u] + flag * sums[units - 1]
    def both(even, odd):
        return jnp.where(half, jnp.broadcast_to(even, (8, particles)), jnp.broadcast_to(odd, (8, particles)))

    def settle(t, carry):
        for j in range(0, rows, 2):
            r = t * rows + j
            p = t * (rows // 2) + j // 2
            lines = []
            for h in (0, 1):
                end = jnp.minimum(ends[r + h], final) - 1
                have = end >= jnp.maximum(begins[r + h], first)
                spot = jnp.where(have, end - first, span)
                last[r + h] = spot
                own = jnp.where(have, selfs[jnp.where(have, end - first, 0)], 0.0)
                twice = geo[t, j + h, 3:4, :] + geo[t, j + h, 3:4, :]
                itself = pltpu.reciprocal(twice, approx=APPROX)
                degree = jnp.sum(sums[spot], axis=0, keepdims=True) - own * itself
                lines.append((degree, own * itself.astype(bf16).astype(f32)))
            mine_deg[p] = both(lines[0][0], lines[1][0])
            corr[p] = both(lines[0][1], lines[1][1])
        return carry

    lax.fori_loop(0, teams, settle, 0)

    def swap(source, place, n):
        return pltpu.make_async_remote_copy(
            src_ref=source, dst_ref=place, send_sem=pair_send.at[n], recv_sem=pair_recv.at[n],
            device_id=partner, device_id_type=MESH,
        )

    degrees = swap(mine_deg, their_deg, 2)
    degrees.start()

    nothing = jnp.zeros((8, particles), f32)

    def publish(p, fresh):
        turned = pltpu.roll(fresh, width, 0)
        for h, line in ((0, jnp.where(half, fresh, turned)), (1, jnp.where(half, turned, fresh))):
            low[2 * p + h] = jnp.concatenate([line, nothing], 0).astype(bf16)
            high[2 * p + h] = jnp.concatenate([nothing, line], 0).astype(bf16)

    for ahead in others:
        gather(3, ahead).wait()
        gather(4, ahead).wait()

    def begin_fields(t, carry):
        for q in range(rows // 4):
            block = landed[t, q].astype(f32)
            for h in (0, 1):
                p = t * (rows // 2) + 2 * q + h
                cur[p] = block[8 * h : 8 * h + 8]
                prev[p] = nothing
                publish(p, block[8 * h : 8 * h + 8])
        return carry

    lax.fori_loop(0, teams, begin_fields, 0)

    def step(k, carry):
        slot = lax.rem(k, 2)

        def unit(u, state):
            taken = jnp.concatenate([low[ids[u]], high[ids[units + u]]], axis=1)
            product = jnp.dot(taken, tiles[u], preferred_element_type=f32)
            zero = state[0] * keep[u] + product[0:8]
            one = state[1] * keep[units + u] + product[8:16]
            parts[u] = zero
            parts[units + u] = one
            return zero, one

        lax.fori_loop(0, units, unit, (blank, blank), unroll=UNROLL)
        for u in range(slots - 1):
            parts[units + u] = parts[units + u] + more[u] * parts[units - 1]

        def pack(p, carry):
            own = cur[p].astype(bf16).astype(f32)
            product = jnp.where(half, parts[last[2 * p]], parts[last[2 * p + 1]])
            mine_sum[slot, p] = product - corr[p] * own
            return carry

        lax.fori_loop(0, pairs, pack, 0, unroll=8)
        exchange = swap(mine_sum.at[slot], their_sum.at[slot], slot)
        exchange.start()

        @pl.when(k == 0)
        def _():
            degrees.wait()

            def divide(t, carry):
                for j in range(0, rows, 2):
                    p = t * (rows // 2) + j // 2
                    exchange = both(fluid[t, j : j + 1, :], fluid[t, j + 1 : j + 2, :])
                    inv[p] = (2.0 / HALF_SPAN) / (exchange + (mine_deg[p] + their_deg[p]))
                return carry

            lax.fori_loop(0, teams, divide, 0)

        exchange.wait()
        gain = jnp.where(k == 0, 0.5, 1.0)

        def update(p, carry):
            field = cur[p]
            product = mine_sum[slot, p] + their_sum[slot, p]
            change = (2.0 * (1.0 - CENTER) / HALF_SPAN) * field - product * inv[p]
            fresh = gain * change - prev[p]
            prev[p] = field
            cur[p] = fresh
            publish(p, fresh)
            return carry

        lax.fori_loop(0, pairs, update, 0, unroll=8)
        return carry

    lax.fori_loop(0, DEGREE, step, 0)

    few = rows // 2

    def deliver(ahead):
        goal = lax.rem(team + ahead, teams)
        return pltpu.make_async_remote_copy(
            src_ref=cur.at[pl.ds(goal * few, few)], dst_ref=arrived.at[team],
            send_sem=gather_send.at[5, ahead], recv_sem=gather_recv.at[5, ahead],
            device_id=at(ahead), device_id_type=MESH,
        )

    for ahead in others:
        deliver(ahead).start()
    for p in range(few):
        arrived[team, p] = cur[team * few + p]
    for ahead in others:
        deliver(ahead).wait()
    for p in range(few):
        for c in range(0, teams, 2):
            one, two = arrived[c, p], arrived[c + 1, p]
            out[2 * p, c * width : c * width + 8, :] = jnp.where(half, one, pltpu.roll(two, width, 0))
            out[2 * p + 1, c * width : c * width + 8, :] = jnp.where(half, pltpu.roll(one, width, 0), two)


def bed(teams, probe, positions, conductivity, fluid_exchange, row_blocks, column_blocks):
    rows, columns, particles = probe.shape
    slots = column_blocks.shape[1]
    clusters = teams * rows
    total = MEAN_BLOCKS * clusters
    units = total // 4
    span = 2 * units
    pairs = clusters // 2
    f32, bf16, i32 = jnp.float32, jnp.bfloat16, jnp.int32
    vmem = pl.BlockSpec(memory_space=pltpu.VMEM)
    anywhere = pl.BlockSpec(memory_space=pl.ANY)
    field = pltpu.VMEM((pairs, 8, particles), f32)
    return pl.pallas_call(
        functools.partial(bed_kernel, teams, total),
        out_shape=jax.ShapeDtypeStruct((rows, columns, particles), f32),
        in_specs=[anywhere] * 6,
        out_specs=vmem,
        scratch_shapes=[
            pltpu.VMEM(probe.shape, probe.dtype),
            pltpu.VMEM(positions.shape, f32),
            pltpu.VMEM(conductivity.shape, f32),
            pltpu.SemaphoreType.DMA((6,)),
            pltpu.VMEM((teams, rows, 4, particles), f32),
            pltpu.VMEM((teams, rows, slots), i32),
            pltpu.VMEM((teams, 1, rows), i32),
            pltpu.SMEM((teams, 1, rows), i32),
            pltpu.SMEM((clusters, slots), i32),
            pltpu.SemaphoreType.DMA((teams + 1,)),
            pltpu.VMEM((teams, rows, particles), f32),
            pltpu.VMEM((teams, rows // 4, 16, particles), bf16),
            pltpu.VMEM((teams, rows // 4, 16, particles), bf16),
            pltpu.VMEM((clusters, 8, particles), f32),
            pltpu.VMEM((clusters, 8, particles), f32),
            pltpu.VMEM((clusters, particles, 32), bf16),
            pltpu.VMEM((clusters, 32, particles), bf16),
            pltpu.VMEM((units, 2 * particles, particles), bf16),
            pltpu.SMEM((clusters + 1,), i32),
            pltpu.SMEM((clusters + 1,), i32),
            pltpu.SMEM((span,), i32),
            pltpu.SMEM((span,), f32),
            pltpu.SMEM((span,), f32),
            pltpu.SMEM((slots,), f32),
            pltpu.SMEM((clusters,), i32),
            pltpu.VMEM((span + 1, 8, particles), f32),
            pltpu.VMEM((span + 1, 8, particles), f32),
            pltpu.VMEM((clusters, 16, particles), bf16),
            pltpu.VMEM((clusters, 16, particles), bf16),
            field, field, field, field,
            pltpu.VMEM((2, pairs, 8, particles), f32),
            pltpu.VMEM((2, pairs, 8, particles), f32),
            field, field,
            pltpu.VMEM((teams, rows // 2, 8, particles), f32),
            pltpu.SemaphoreType.DMA((6, teams)),
            pltpu.SemaphoreType.DMA((6, teams)),
            pltpu.SemaphoreType.DMA((3,)),
            pltpu.SemaphoreType.DMA((3,)),
        ],
        compiler_params=pltpu.CompilerParams(
            collective_id=1, has_side_effects=True, vmem_limit_bytes=60 * 1024 * 1024
        ),
    )(probe, positions, conductivity, fluid_exchange, row_blocks.reshape(1, rows), column_blocks)


def either(teams, probe, *rest):
    rows, columns, particles = probe.shape
    if columns == 4 * teams and rows % 4 == 0 and MEAN_BLOCKS * teams * rows <= 1024:
        return bed(teams, probe, *rest)
    return local(teams, probe, *rest)


def solution(mesh):
    return jax.shard_map(
        functools.partial(either, mesh.shape["blk"]),
        mesh=mesh,
        in_specs=(
            P(("groups", "blk"), None, None),
            P(("groups", "blk"), None, None),
            P(("groups", "blk"), None),
            P(("groups", "blk"), None),
            P(("groups", "blk")),
            P(("groups", "blk"), None),
        ),
        out_specs=P(("groups", "blk"), None, None),
        check_vma=False,
    )
```

```python
import functools
import math

import jax
import jax.numpy as jnp
from jax import lax
from jax.experimental import pallas as pl
from jax.experimental.pallas import tpu as pltpu
from jax.sharding import PartitionSpec as P

DEGREE = 8
WIDTH_SQ = 0.245
CENTER = 1.05
HALF_SPAN = 0.95
SCALE = math.sqrt(math.log2(math.e) / WIDTH_SQ)
MESH = pl.DeviceIdType.MESH
REACHES = (-2, -1, 1, 2)
CHUNK = 3
MEAN_BLOCKS = 9
APPROX = True
UNROLL = 216
BUILD = 24
PIECES = 2
SPREAD = 12


def kernel(
    teams, probe_in, pos_in, cond_in, fluid_in, counts_in, cols_in, out,
    probe, pos, cond, fluid, counts, cols, load_sem,
    geo, bcast, tiles, even, odd, cur, prev, inv, corr, ids, other,
    geo_send, geo_recv, win_send, win_recv, pair_send, pair_recv,
):
    loads = [
        pltpu.make_async_copy(source, place, load_sem.at[n])
        for n, (source, place) in enumerate(
            (
                (pos_in, pos), (cond_in, cond), (probe_in, probe),
                (cols_in, cols), (counts_in, counts), (fluid_in, fluid),
            )
        )
    ]
    for load in loads:
        load.start()
    rows, columns, particles = probe.shape
    half = columns // 2
    slots = cols.shape[1]
    clusters = teams * rows
    group = lax.axis_index("groups")
    member = lax.axis_index("team")
    team = lax.axis_index("blk")

    def at(reach):
        return (group, member, lax.rem(team + reach + teams, teams))

    partner = (group, 1 - member, team)
    barrier = pltpu.get_barrier_semaphore()
    for reach in REACHES:
        pl.semaphore_signal(barrier, inc=1, device_id=at(reach), device_id_type=MESH)
    pl.semaphore_signal(barrier, inc=1, device_id=partner, device_id_type=MESH)

    for load in loads[:3]:
        load.wait()
    for r in range(rows):
        geo[2, r, 0:3, :] = pos[r] * SCALE
        geo[2, r, 3:4, :] = 0.5 / cond[r : r + 1, :]
        mine = probe[r, pl.ds(pl.multiple_of(member * half, half), half), :]
        even[2 * rows + r] = mine
        cur[r] = mine.astype(jnp.float32)
        prev[r] = jnp.zeros((half, particles), jnp.float32)
    pl.semaphore_wait(barrier, len(REACHES) + 1)

    def geo_copy(n):
        reach = REACHES[n]
        return pltpu.make_async_remote_copy(
            src_ref=geo.at[2], dst_ref=geo.at[2 - reach],
            send_sem=geo_send.at[n], recv_sem=geo_recv.at[n],
            device_id=at(reach), device_id_type=MESH,
        )

    def win_copy(parity, n, first=0, size=None):
        reach = REACHES[n]
        window = (even, odd)[parity]
        size = rows if size is None else size
        return pltpu.make_async_remote_copy(
            src_ref=window.at[pl.ds(2 * rows + first, size)], dst_ref=window.at[pl.ds((2 - reach) * rows + first, size)],
            send_sem=win_send.at[parity, n], recv_sem=win_recv.at[parity, n],
            device_id=at(reach), device_id_type=MESH,
        )

    for n in range(4):
        geo_copy(n).start()
    def spread(place):
        def one(r, carry):
            for k in range(4):
                line = geo[place, r, k : k + 1, :]
                bcast[place * rows + r, k] = jnp.broadcast_to(line, (particles, particles)).T
            return carry
        lax.fori_loop(0, rows, one, 0, unroll=2)

    spread(2)
    for n in range(4):
        geo_copy(n).wait()
        spread(2 - REACHES[n])
    for n in range(4):
        win_copy(0, n).start()

    for load in loads[3:]:
        load.wait()
    base = (team - 2) * rows

    def build_row(r, carry):
        own = team * rows + r
        count = counts[r]
        xi = [jnp.broadcast_to(geo[2, r, k : k + 1, :], (8, particles)) for k in range(4)]

        def build_tile(s, state):
            total, selves = state
            col = cols[r, s]
            active = s < count
            place = col - base
            place = jnp.where(place < 0, place + clusters, place)
            place = jnp.where(place >= clusters, place - clusters, place)
            place = jnp.where(active, jnp.minimum(place, 5 * rows - 1), 0)
            ids[r, s] = place
            selves = selves + jnp.where(active & (col == own), 1.0, 0.0)
            bias = jnp.where(active, 0.0, -1e30)
            for j in range(0, particles, 16):
                parts = []
                for h in (j, j + 8):
                    dx = bcast[place, 0, h : h + 8, :] - xi[0]
                    dy = bcast[place, 1, h : h + 8, :] - xi[1]
                    dz = bcast[place, 2, h : h + 8, :] - xi[2]
                    power = bias - dx * dx - dy * dy - dz * dz
                    value = jnp.exp2(power) / (bcast[place, 3, h : h + 8, :] + xi[3])
                    total = total + value
                    parts.append(value)
                tiles[r, pl.ds(pl.multiple_of(s * particles + j, 16), 16), :] = jnp.concatenate(
                    parts, 0
                ).astype(jnp.bfloat16)
            return total, selves

        total, selves = lax.fori_loop(
            0, slots, build_tile, (jnp.zeros((8, particles), jnp.float32), jnp.float32(0.0)),
            unroll=3,
        )
        itself = 1.0 / (xi[3] + xi[3])
        degree = jnp.sum(total, axis=0, keepdims=True) - selves * itself[0:1]
        divisor = fluid[pl.ds(r, 1), :] + degree
        inv[r] = jnp.broadcast_to((2.0 / HALF_SPAN) / divisor, (half, particles))
        rounded = itself[0:1].astype(jnp.bfloat16).astype(jnp.float32)
        corr[r] = jnp.broadcast_to(selves * rounded, (half, particles))
        return carry

    lax.fori_loop(0, rows, build_row, 0)

    def step(k, now):
        later = 1 - now
        window, target = (even, odd)[now], (even, odd)[later]
        for n in range(4):
            win_copy(now, n).wait()
        gain = jnp.where(k == 0, 0.5, 1.0)

        def row(r):
            taken = jnp.concatenate(
                [window[ids[r, s]] for s in range(slots)],
                axis=1,
            )
            product = jnp.dot(taken, tiles[r], preferred_element_type=jnp.float32)
            mine = window[2 * rows + r].astype(jnp.float32)
            product = product - corr[r] * mine
            field = cur[r]
            change = (2.0 * (1.0 - CENTER) / HALF_SPAN) * field - product * inv[r]
            fresh = gain * change - prev[r]
            prev[r] = field
            cur[r] = fresh
            target[2 * rows + r] = fresh.astype(jnp.bfloat16)

        for first in range(0, rows, CHUNK):
            size = min(CHUNK, rows - first)
            for r in range(first, first + size):
                row(r)

            @pl.when(k < DEGREE - 1)
            def _():
                for n in range(4):
                    win_copy(later, n, first, size).start()

    def two_steps(i, carry):
        step(2 * i, 0)
        step(2 * i + 1, 1)
        return carry

    lax.fori_loop(0, DEGREE // 2, two_steps, 0)

    swap = pltpu.make_async_remote_copy(
        src_ref=cur, dst_ref=other, send_sem=pair_send, recv_sem=pair_recv,
        device_id=partner, device_id_type=MESH,
    )
    swap.start()
    out[:, pl.ds(pl.multiple_of(member * half, half), half), :] = cur[...]
    swap.wait()
    out[:, pl.ds(pl.multiple_of((1 - member) * half, half), half), :] = other[...]


def local(teams, probe, positions, conductivity, fluid_exchange, row_blocks, column_blocks):
    rows, columns, particles = probe.shape
    slots = column_blocks.shape[1]
    half = columns // 2
    vmem = pl.BlockSpec(memory_space=pltpu.VMEM)
    anywhere = pl.BlockSpec(memory_space=pl.ANY)
    f32 = jnp.float32
    return pl.pallas_call(
        functools.partial(kernel, teams),
        out_shape=jax.ShapeDtypeStruct((rows, columns, particles), f32),
        in_specs=[anywhere] * 6,
        out_specs=vmem,
        scratch_shapes=[
            pltpu.VMEM(probe.shape, probe.dtype),
            pltpu.VMEM(positions.shape, f32),
            pltpu.VMEM(conductivity.shape, f32),
            pltpu.VMEM(fluid_exchange.shape, f32),
            pltpu.SMEM(row_blocks.shape, jnp.int32),
            pltpu.SMEM(column_blocks.shape, jnp.int32),
            pltpu.SemaphoreType.DMA((6,)),
            pltpu.VMEM((5, rows, 4, particles), f32),
            pltpu.VMEM((5 * rows, 4, particles, particles), f32),
            pltpu.VMEM((rows, slots * particles, particles), jnp.bfloat16),
            pltpu.VMEM((5 * rows, half, particles), jnp.bfloat16),
            pltpu.VMEM((5 * rows, half, particles), jnp.bfloat16),
            pltpu.VMEM((rows, half, particles), f32),
            pltpu.VMEM((rows, half, particles), f32),
            pltpu.VMEM((rows, half, particles), f32),
            pltpu.VMEM((rows, half, particles), f32),
            pltpu.SMEM((rows, slots), jnp.int32),
            pltpu.VMEM((rows, half, particles), f32),
            pltpu.SemaphoreType.DMA((4,)),
            pltpu.SemaphoreType.DMA((4,)),
            pltpu.SemaphoreType.DMA((2, 4)),
            pltpu.SemaphoreType.DMA((2, 4)),
            pltpu.SemaphoreType.DMA,
            pltpu.SemaphoreType.DMA,
        ],
        compiler_params=pltpu.CompilerParams(
            collective_id=0, has_side_effects=True, vmem_limit_bytes=60 * 1024 * 1024
        ),
    )(probe, positions, conductivity, fluid_exchange, row_blocks, column_blocks)


def bed_kernel(
    teams, total, probe_in, pos_in, cond_in, fluid_in, counts_in, cols_in, out,
    probe, pos, cond, load_sem,
    geo, ints, cnts, counts, cols, smem_sem, fluid, stage, landed,
    points, mid, lines, flank, tiles, ends, begins, ids, keep, selfs, more, last,
    sums, parts, low, high, cur, prev, inv, corr, mine_sum, their_sum, mine_deg, their_deg, arrived,
    gather_send, gather_recv, pair_send, pair_recv,
):
    rows, columns, particles = probe.shape
    slots = cols.shape[1]
    clusters = teams * rows
    width = columns // teams
    pairs = clusters // 2
    units = tiles.shape[0]
    span = 2 * units
    group = lax.axis_index("groups")
    member = lax.axis_index("team")
    team = lax.axis_index("blk")
    f32, bf16 = jnp.float32, jnp.bfloat16

    def at(ahead):
        return (group, member, lax.rem(team + ahead, teams))

    partner = (group, 1 - member, team)
    barrier = pltpu.get_barrier_semaphore()
    for ahead in range(1, teams):
        pl.semaphore_signal(barrier, inc=1, device_id=at(ahead), device_id_type=MESH)
    pl.semaphore_signal(barrier, inc=1, device_id=partner, device_id_type=MESH)

    loads = [
        pltpu.make_async_copy(source, place, load_sem.at[n])
        for n, (source, place) in enumerate(
            (
                (pos_in, pos), (cond_in, cond), (probe_in, probe),
                (cols_in, cols.at[pl.ds(team * rows, rows)]), (counts_in, counts.at[team]), (fluid_in, fluid.at[team]),
            )
        )
    ]
    for load in loads:
        load.start()
    for load in loads[:2]:
        load.wait()
    for r in range(rows):
        geo[team, r, 0:3, :] = pos[r] * SCALE
        geo[team, r, 3:4, :] = 0.5 / cond[r : r + 1, :]
    pl.semaphore_wait(barrier, teams)

    def gather(kind, ahead):
        source, place = (
            (counts.at[team], counts.at[team]), (cols.at[pl.ds(team * rows, rows)], cols.at[pl.ds(team * rows, rows)]), (geo.at[team], geo.at[team]),
            (stage.at[lax.rem(team + ahead, teams)], landed.at[team]), (fluid_in, fluid.at[team]),
        )[kind]
        return pltpu.make_async_remote_copy(
            src_ref=source, dst_ref=place,
            send_sem=gather_send.at[kind, ahead], recv_sem=gather_recv.at[kind, ahead],
            device_id=at(ahead), device_id_type=MESH,
        )

    others = range(1, teams)
    for load in loads[3:5]:
        load.wait()
    for ahead in others:
        gather(0, ahead).start()
        gather(1, ahead).start()
    for ahead in others:
        gather(2, ahead).start()

    level = lax.broadcasted_iota(jnp.int32, (8, particles), 0)
    half = level < width
    square = level % width == 3

    def rounded(value):
        return value.astype(bf16).astype(f32)

    def thirds(value):
        head = rounded(value)
        tail = value - head
        body = rounded(tail)
        return head, body, tail - body

    def length(value):
        value = value * value
        value = value + pltpu.roll(value, 1, 0)
        return value + pltpu.roll(value, 2, 0)

    def spread(place):
        def one(r, carry):
            spot = place * rows + r
            point = geo[place, r]
            point = jnp.where(square, 0.0, jnp.concatenate([point, point], 0))
            middle = jnp.broadcast_to(jnp.sum(point * (1.0 / particles), axis=1, keepdims=True), (8, particles))
            points[spot] = point
            mid[spot] = middle
            off = point - middle
            a, b, c = thirds(off)
            d, e, f = thirds(length(off))
            g, h, i = thirds(jnp.broadcast_to(geo[place, r, 3:4, :], (8, particles)))
            last_line = jnp.zeros((8, particles), f32)
            for n, value in enumerate((d, e, f, g, h, i)):
                last_line = jnp.where(level == n, value, last_line)
            block = jnp.concatenate(
                [
                    jnp.where(level == 3, 1.0, jnp.where(half, a, b)),
                    jnp.where(level == 7, 1.0, jnp.where(half, c, a)),
                    jnp.where(level == 7, 1.0, jnp.where(half, b, a)),
                    last_line,
                ],
                0,
            )
            lines[spot] = block.astype(bf16).T
            flank[spot] = jnp.concatenate(
                [
                    jnp.where(level == 3, g, 0.0),
                    jnp.where(level == 7, h, 0.0),
                    jnp.where(level == 7, i, 0.0),
                    jnp.where((level > 2) & (level < 6), 1.0, 0.0),
                ],
                0,
            ).astype(bf16)
            return carry
        lax.fori_loop(0, rows, one, 0, unroll=SPREAD)

    spread(team)
    loads[2].wait()
    loads[5].wait()
    for q in range(rows // 4):
        wide = [probe[4 * q + a].astype(f32) for a in range(4)]
        for t in range(teams):
            stage[t, q] = jnp.concatenate([w[t * width : (t + 1) * width] for w in wide], 0).astype(bf16)
    landed[team] = stage[team]
    for ahead in others:
        gather(0, ahead).wait()
        gather(1, ahead).wait()
    first = member * span
    final = first + span

    def lay(t, state):
        at_end, zero, one = state
        for j in range(rows):
            r = t * rows + j
            begins[r] = at_end
            at_end = at_end + counts[t, 0, j]
            ends[r] = at_end
            zero = zero + jnp.where(at_end <= first, 1, 0)
            one = one + jnp.where(at_end <= first + units, 1, 0)
        return at_end, zero, one

    _, zero, one = lax.fori_loop(0, teams, lay, (jnp.int32(0), jnp.int32(0), jnp.int32(0)))
    zero, one = jnp.minimum(zero, clusters - 1), jnp.minimum(one, clusters - 1)

    for ahead in others:
        gather(2, ahead).wait()
        spread(lax.rem(team + teams - ahead, teams))
    for ahead in others:
        gather(3, ahead).start()
        gather(4, ahead).start()


    ones = jnp.where(level < 3, 1.0, 0.0)

    def build_tile(u, lane, r, selves, running):
        place = first + lane * units + u
        index = lane * units + u
        r = jnp.minimum(r + jnp.where(place >= ends[r], 1, 0), clusters - 1)
        begin = begins[r]
        col = cols[r, jnp.minimum(place - begin, slots - 1)]
        fresh = jnp.logical_or(place == begin, u == 0)
        going = jnp.where(fresh, 0.0, 1.0)
        ids[index] = col
        keep[index] = going
        selves = jnp.where(fresh, 0.0, selves) + jnp.where(col == r, 1.0, 0.0)
        selfs[index] = selves
        off = points[r] - mid[col]
        a, b, c = thirds(jnp.where(square, length(off), -2.0 * off))
        block = jnp.concatenate([a, jnp.where(half, a, b), jnp.where(half, b, c), ones], 0).astype(bf16)
        both_sides = jnp.dot(
            lines[col], jnp.concatenate([block, flank[r]], 1), preferred_element_type=f32
        )
        tally = jnp.zeros((8, particles), f32)
        for j in range(0, particles, 16):
            values = []
            for h in (j, j + 8):
                power = both_sides[h : h + 8, :particles]
                value = pltpu.reciprocal(both_sides[h : h + 8, particles:] * jnp.exp2(power), approx=APPROX)
                tally = tally + value
                values.append(value)
            tiles[u, lane * particles + j : lane * particles + j + 16, :] = jnp.concatenate(values, 0).astype(bf16)
        running = running * going + tally
        sums[index] = running
        return r, selves, running

    def build(u, state):
        return build_tile(u, 0, *state[:3]) + build_tile(u, 1, *state[3:])

    blank = jnp.zeros((8, particles), f32)
    state = lax.fori_loop(
        0, units, build, (zero, jnp.float32(0.0), blank, one, jnp.float32(0.0), blank), unroll=BUILD
    )

    sums[span] = blank
    parts[span] = blank
    edge_row = state[0]
    edge = ends[edge_row]
    for u in range(slots - 1):
        flag = jnp.where(first + units + u < edge, 1.0, 0.0)
        more[u] = flag
        selfs[units + u] = selfs[units + u] + flag * selfs[units - 1]
        sums[units + u] = sums[units + u] + flag * sums[units - 1]
    def both(even, odd):
        return jnp.where(half, jnp.broadcast_to(even, (8, particles)), jnp.broadcast_to(odd, (8, particles)))

    def settle(t, carry):
        for j in range(0, rows, 2):
            r = t * rows + j
            p = t * (rows // 2) + j // 2
            lines = []
            for h in (0, 1):
                end = jnp.minimum(ends[r + h], final) - 1
                have = end >= jnp.maximum(begins[r + h], first)
                spot = jnp.where(have, end - first, span)
                last[r + h] = spot
                own = jnp.where(have, selfs[jnp.where(have, end - first, 0)], 0.0)
                twice = geo[t, j + h, 3:4, :] + geo[t, j + h, 3:4, :]
                itself = pltpu.reciprocal(twice, approx=APPROX)
                degree = jnp.sum(sums[spot], axis=0, keepdims=True) - own * itself
                lines.append((degree, own * itself.astype(bf16).astype(f32)))
            mine_deg[p] = both(lines[0][0], lines[1][0])
            corr[p] = both(lines[0][1], lines[1][1])
        return carry

    lax.fori_loop(0, teams, settle, 0)

    def swap(source, place, n):
        return pltpu.make_async_remote_copy(
            src_ref=source, dst_ref=place, send_sem=pair_send.at[n], recv_sem=pair_recv.at[n],
            device_id=partner, device_id_type=MESH,
        )

    degrees = swap(mine_deg, their_deg, 2)
    degrees.start()

    nothing = jnp.zeros((8, particles), f32)

    def publish(p, fresh):
        turned = pltpu.roll(fresh, width, 0)
        for h, line in ((0, jnp.where(half, fresh, turned)), (1, jnp.where(half, turned, fresh))):
            low[2 * p + h] = jnp.concatenate([line, nothing], 0).astype(bf16)
            high[2 * p + h] = jnp.concatenate([nothing, line], 0).astype(bf16)

    for ahead in others:
        gather(3, ahead).wait()
        gather(4, ahead).wait()

    def begin_fields(t, carry):
        for q in range(rows // 4):
            block = landed[t, q].astype(f32)
            for h in (0, 1):
                p = t * (rows // 2) + 2 * q + h
                cur[p] = block[8 * h : 8 * h + 8]
                prev[p] = nothing
                publish(p, block[8 * h : 8 * h + 8])
        return carry

    lax.fori_loop(0, teams, begin_fields, 0)

    def step(k, carry):
        slot = lax.rem(k, 2)

        def unit(u, state):
            taken = jnp.concatenate([low[ids[u]], high[ids[units + u]]], axis=1)
            product = jnp.dot(taken, tiles[u], preferred_element_type=f32)
            zero = state[0] * keep[u] + product[0:8]
            one = state[1] * keep[units + u] + product[8:16]
            parts[u] = zero
            parts[units + u] = one
            return zero, one

        lax.fori_loop(0, units, unit, (blank, blank), unroll=UNROLL)
        for u in range(slots - 1):
            parts[units + u] = parts[units + u] + more[u] * parts[units - 1]

        def pack(p, carry):
            own = cur[p].astype(bf16).astype(f32)
            product = jnp.where(half, parts[last[2 * p]], parts[last[2 * p + 1]])
            mine_sum[slot, p] = product - corr[p] * own
            return carry

        share = pairs // PIECES
        exchanges = [
            swap(
                mine_sum.at[slot, pl.ds(n * share, share)], their_sum.at[slot, pl.ds(n * share, share)],
                3 + 2 * n + slot,
            )
            for n in range(PIECES)
        ]
        for n in range(PIECES):
            lax.fori_loop(n * share, (n + 1) * share, pack, 0, unroll=8)
            exchanges[n].start()

        @pl.when(k == 0)
        def _():
            degrees.wait()

            def divide(t, carry):
                for j in range(0, rows, 2):
                    p = t * (rows // 2) + j // 2
                    exchange = both(fluid[t, j : j + 1, :], fluid[t, j + 1 : j + 2, :])
                    inv[p] = (2.0 / HALF_SPAN) / (exchange + (mine_deg[p] + their_deg[p]))
                return carry

            lax.fori_loop(0, teams, divide, 0)

        gain = jnp.where(k == 0, 0.5, 1.0)

        def update(p, carry):
            field = cur[p]
            product = mine_sum[slot, p] + their_sum[slot, p]
            change = (2.0 * (1.0 - CENTER) / HALF_SPAN) * field - product * inv[p]
            fresh = gain * change - prev[p]
            prev[p] = field
            cur[p] = fresh
            publish(p, fresh)
            return carry

        for n in range(PIECES):
            exchanges[n].wait()
            lax.fori_loop(n * share, (n + 1) * share, update, 0, unroll=8)
        return carry

    lax.fori_loop(0, DEGREE, step, 0)

    few = rows // 2

    def deliver(ahead):
        goal = lax.rem(team + ahead, teams)
        return pltpu.make_async_remote_copy(
            src_ref=cur.at[pl.ds(goal * few, few)], dst_ref=arrived.at[team],
            send_sem=gather_send.at[5, ahead], recv_sem=gather_recv.at[5, ahead],
            device_id=at(ahead), device_id_type=MESH,
        )

    for ahead in others:
        deliver(ahead).start()
    for p in range(few):
        arrived[team, p] = cur[team * few + p]
    for ahead in others:
        deliver(ahead).wait()
    for p in range(few):
        for c in range(0, teams, 2):
            one, two = arrived[c, p], arrived[c + 1, p]
            out[2 * p, c * width : c * width + 8, :] = jnp.where(half, one, pltpu.roll(two, width, 0))
            out[2 * p + 1, c * width : c * width + 8, :] = jnp.where(half, pltpu.roll(one, width, 0), two)


def bed(teams, probe, positions, conductivity, fluid_exchange, row_blocks, column_blocks):
    rows, columns, particles = probe.shape
    slots = column_blocks.shape[1]
    clusters = teams * rows
    total = MEAN_BLOCKS * clusters
    units = total // 4
    span = 2 * units
    pairs = clusters // 2
    f32, bf16, i32 = jnp.float32, jnp.bfloat16, jnp.int32
    vmem = pl.BlockSpec(memory_space=pltpu.VMEM)
    anywhere = pl.BlockSpec(memory_space=pl.ANY)
    field = pltpu.VMEM((pairs, 8, particles), f32)
    return pl.pallas_call(
        functools.partial(bed_kernel, teams, total),
        out_shape=jax.ShapeDtypeStruct((rows, columns, particles), f32),
        in_specs=[anywhere] * 6,
        out_specs=vmem,
        scratch_shapes=[
            pltpu.VMEM(probe.shape, probe.dtype),
            pltpu.VMEM(positions.shape, f32),
            pltpu.VMEM(conductivity.shape, f32),
            pltpu.SemaphoreType.DMA((6,)),
            pltpu.VMEM((teams, rows, 4, particles), f32),
            pltpu.VMEM((teams, rows, slots), i32),
            pltpu.VMEM((teams, 1, rows), i32),
            pltpu.SMEM((teams, 1, rows), i32),
            pltpu.SMEM((clusters, slots), i32),
            pltpu.SemaphoreType.DMA((teams + 1,)),
            pltpu.VMEM((teams, rows, particles), f32),
            pltpu.VMEM((teams, rows // 4, 16, particles), bf16),
            pltpu.VMEM((teams, rows // 4, 16, particles), bf16),
            pltpu.VMEM((clusters, 8, particles), f32),
            pltpu.VMEM((clusters, 8, particles), f32),
            pltpu.VMEM((clusters, particles, 32), bf16),
            pltpu.VMEM((clusters, 32, particles), bf16),
            pltpu.VMEM((units, 2 * particles, particles), bf16),
            pltpu.SMEM((clusters + 1,), i32),
            pltpu.SMEM((clusters + 1,), i32),
            pltpu.SMEM((span,), i32),
            pltpu.SMEM((span,), f32),
            pltpu.SMEM((span,), f32),
            pltpu.SMEM((slots,), f32),
            pltpu.SMEM((clusters,), i32),
            pltpu.VMEM((span + 1, 8, particles), f32),
            pltpu.VMEM((span + 1, 8, particles), f32),
            pltpu.VMEM((clusters, 16, particles), bf16),
            pltpu.VMEM((clusters, 16, particles), bf16),
            field, field, field, field,
            pltpu.VMEM((2, pairs, 8, particles), f32),
            pltpu.VMEM((2, pairs, 8, particles), f32),
            field, field,
            pltpu.VMEM((teams, rows // 2, 8, particles), f32),
            pltpu.SemaphoreType.DMA((6, teams)),
            pltpu.SemaphoreType.DMA((6, teams)),
            pltpu.SemaphoreType.DMA((3 + 2 * PIECES,)),
            pltpu.SemaphoreType.DMA((3 + 2 * PIECES,)),
        ],
        compiler_params=pltpu.CompilerParams(
            collective_id=1, has_side_effects=True, vmem_limit_bytes=60 * 1024 * 1024
        ),
    )(probe, positions, conductivity, fluid_exchange, row_blocks.reshape(1, rows), column_blocks)


def either(teams, probe, *rest):
    rows, columns, particles = probe.shape
    if columns == 4 * teams and rows % 4 == 0 and MEAN_BLOCKS * teams * rows <= 1024:
        return bed(teams, probe, *rest)
    return local(teams, probe, *rest)


def solution(mesh):
    return jax.shard_map(
        functools.partial(either, mesh.shape["blk"]),
        mesh=mesh,
        in_specs=(
            P(("groups", "blk"), None, None),
            P(("groups", "blk"), None, None),
            P(("groups", "blk"), None),
            P(("groups", "blk"), None),
            P(("groups", "blk")),
            P(("groups", "blk"), None),
        ),
        out_specs=P(("groups", "blk"), None, None),
        check_vma=False,
    )
```

```python
import functools
import math

import jax
import jax.numpy as jnp
from jax import lax
from jax.experimental import pallas as pl
from jax.experimental.pallas import tpu as pltpu
from jax.sharding import PartitionSpec as P

DEGREE = 8
WIDTH_SQ = 0.245
CENTER = 1.05
HALF_SPAN = 0.95
SCALE = math.sqrt(math.log2(math.e) / WIDTH_SQ)
MESH = pl.DeviceIdType.MESH
REACHES = (-2, -1, 1, 2)
CHUNK = 3
MEAN_BLOCKS = 9
APPROX = True
UNROLL = 216
BUILD = 54
PIECES = 2
SPREAD = 12


def kernel(
    teams, probe_in, pos_in, cond_in, fluid_in, counts_in, cols_in, out,
    probe, pos, cond, fluid, counts, cols, load_sem,
    geo, bcast, tiles, even, odd, cur, prev, inv, corr, ids, other,
    geo_send, geo_recv, win_send, win_recv, pair_send, pair_recv,
):
    loads = [
        pltpu.make_async_copy(source, place, load_sem.at[n])
        for n, (source, place) in enumerate(
            (
                (pos_in, pos), (cond_in, cond), (probe_in, probe),
                (cols_in, cols), (counts_in, counts), (fluid_in, fluid),
            )
        )
    ]
    for load in loads:
        load.start()
    rows, columns, particles = probe.shape
    half = columns // 2
    slots = cols.shape[1]
    clusters = teams * rows
    group = lax.axis_index("groups")
    member = lax.axis_index("team")
    team = lax.axis_index("blk")

    def at(reach):
        return (group, member, lax.rem(team + reach + teams, teams))

    partner = (group, 1 - member, team)
    barrier = pltpu.get_barrier_semaphore()
    for reach in REACHES:
        pl.semaphore_signal(barrier, inc=1, device_id=at(reach), device_id_type=MESH)
    pl.semaphore_signal(barrier, inc=1, device_id=partner, device_id_type=MESH)

    for load in loads[:3]:
        load.wait()
    for r in range(rows):
        geo[2, r, 0:3, :] = pos[r] * SCALE
        geo[2, r, 3:4, :] = 0.5 / cond[r : r + 1, :]
        mine = probe[r, pl.ds(pl.multiple_of(member * half, half), half), :]
        even[2 * rows + r] = mine
        cur[r] = mine.astype(jnp.float32)
        prev[r] = jnp.zeros((half, particles), jnp.float32)
    pl.semaphore_wait(barrier, len(REACHES) + 1)

    def geo_copy(n):
        reach = REACHES[n]
        return pltpu.make_async_remote_copy(
            src_ref=geo.at[2], dst_ref=geo.at[2 - reach],
            send_sem=geo_send.at[n], recv_sem=geo_recv.at[n],
            device_id=at(reach), device_id_type=MESH,
        )

    def win_copy(parity, n, first=0, size=None):
        reach = REACHES[n]
        window = (even, odd)[parity]
        size = rows if size is None else size
        return pltpu.make_async_remote_copy(
            src_ref=window.at[pl.ds(2 * rows + first, size)], dst_ref=window.at[pl.ds((2 - reach) * rows + first, size)],
            send_sem=win_send.at[parity, n], recv_sem=win_recv.at[parity, n],
            device_id=at(reach), device_id_type=MESH,
        )

    for n in range(4):
        geo_copy(n).start()
    def spread(place):
        def one(r, carry):
            for k in range(4):
                line = geo[place, r, k : k + 1, :]
                bcast[place * rows + r, k] = jnp.broadcast_to(line, (particles, particles)).T
            return carry
        lax.fori_loop(0, rows, one, 0, unroll=2)

    spread(2)
    for n in range(4):
        geo_copy(n).wait()
        spread(2 - REACHES[n])
    for n in range(4):
        win_copy(0, n).start()

    for load in loads[3:]:
        load.wait()
    base = (team - 2) * rows

    def build_row(r, carry):
        own = team * rows + r
        count = counts[r]
        xi = [jnp.broadcast_to(geo[2, r, k : k + 1, :], (8, particles)) for k in range(4)]

        def build_tile(s, state):
            total, selves = state
            col = cols[r, s]
            active = s < count
            place = col - base
            place = jnp.where(place < 0, place + clusters, place)
            place = jnp.where(place >= clusters, place - clusters, place)
            place = jnp.where(active, jnp.minimum(place, 5 * rows - 1), 0)
            ids[r, s] = place
            selves = selves + jnp.where(active & (col == own), 1.0, 0.0)
            bias = jnp.where(active, 0.0, -1e30)
            for j in range(0, particles, 16):
                parts = []
                for h in (j, j + 8):
                    dx = bcast[place, 0, h : h + 8, :] - xi[0]
                    dy = bcast[place, 1, h : h + 8, :] - xi[1]
                    dz = bcast[place, 2, h : h + 8, :] - xi[2]
                    power = bias - dx * dx - dy * dy - dz * dz
                    value = jnp.exp2(power) / (bcast[place, 3, h : h + 8, :] + xi[3])
                    total = total + value
                    parts.append(value)
                tiles[r, pl.ds(pl.multiple_of(s * particles + j, 16), 16), :] = jnp.concatenate(
                    parts, 0
                ).astype(jnp.bfloat16)
            return total, selves

        total, selves = lax.fori_loop(
            0, slots, build_tile, (jnp.zeros((8, particles), jnp.float32), jnp.float32(0.0)),
            unroll=3,
        )
        itself = 1.0 / (xi[3] + xi[3])
        degree = jnp.sum(total, axis=0, keepdims=True) - selves * itself[0:1]
        divisor = fluid[pl.ds(r, 1), :] + degree
        inv[r] = jnp.broadcast_to((2.0 / HALF_SPAN) / divisor, (half, particles))
        rounded = itself[0:1].astype(jnp.bfloat16).astype(jnp.float32)
        corr[r] = jnp.broadcast_to(selves * rounded, (half, particles))
        return carry

    lax.fori_loop(0, rows, build_row, 0)

    def step(k, now):
        later = 1 - now
        window, target = (even, odd)[now], (even, odd)[later]
        for n in range(4):
            win_copy(now, n).wait()
        gain = jnp.where(k == 0, 0.5, 1.0)

        def row(r):
            taken = jnp.concatenate(
                [window[ids[r, s]] for s in range(slots)],
                axis=1,
            )
            product = jnp.dot(taken, tiles[r], preferred_element_type=jnp.float32)
            mine = window[2 * rows + r].astype(jnp.float32)
            product = product - corr[r] * mine
            field = cur[r]
            change = (2.0 * (1.0 - CENTER) / HALF_SPAN) * field - product * inv[r]
            fresh = gain * change - prev[r]
            prev[r] = field
            cur[r] = fresh
            target[2 * rows + r] = fresh.astype(jnp.bfloat16)

        for first in range(0, rows, CHUNK):
            size = min(CHUNK, rows - first)
            for r in range(first, first + size):
                row(r)

            @pl.when(k < DEGREE - 1)
            def _():
                for n in range(4):
                    win_copy(later, n, first, size).start()

    def two_steps(i, carry):
        step(2 * i, 0)
        step(2 * i + 1, 1)
        return carry

    lax.fori_loop(0, DEGREE // 2, two_steps, 0)

    swap = pltpu.make_async_remote_copy(
        src_ref=cur, dst_ref=other, send_sem=pair_send, recv_sem=pair_recv,
        device_id=partner, device_id_type=MESH,
    )
    swap.start()
    out[:, pl.ds(pl.multiple_of(member * half, half), half), :] = cur[...]
    swap.wait()
    out[:, pl.ds(pl.multiple_of((1 - member) * half, half), half), :] = other[...]


def local(teams, probe, positions, conductivity, fluid_exchange, row_blocks, column_blocks):
    rows, columns, particles = probe.shape
    slots = column_blocks.shape[1]
    half = columns // 2
    vmem = pl.BlockSpec(memory_space=pltpu.VMEM)
    anywhere = pl.BlockSpec(memory_space=pl.ANY)
    f32 = jnp.float32
    return pl.pallas_call(
        functools.partial(kernel, teams),
        out_shape=jax.ShapeDtypeStruct((rows, columns, particles), f32),
        in_specs=[anywhere] * 6,
        out_specs=vmem,
        scratch_shapes=[
            pltpu.VMEM(probe.shape, probe.dtype),
            pltpu.VMEM(positions.shape, f32),
            pltpu.VMEM(conductivity.shape, f32),
            pltpu.VMEM(fluid_exchange.shape, f32),
            pltpu.SMEM(row_blocks.shape, jnp.int32),
            pltpu.SMEM(column_blocks.shape, jnp.int32),
            pltpu.SemaphoreType.DMA((6,)),
            pltpu.VMEM((5, rows, 4, particles), f32),
            pltpu.VMEM((5 * rows, 4, particles, particles), f32),
            pltpu.VMEM((rows, slots * particles, particles), jnp.bfloat16),
            pltpu.VMEM((5 * rows, half, particles), jnp.bfloat16),
            pltpu.VMEM((5 * rows, half, particles), jnp.bfloat16),
            pltpu.VMEM((rows, half, particles), f32),
            pltpu.VMEM((rows, half, particles), f32),
            pltpu.VMEM((rows, half, particles), f32),
            pltpu.VMEM((rows, half, particles), f32),
            pltpu.SMEM((rows, slots), jnp.int32),
            pltpu.VMEM((rows, half, particles), f32),
            pltpu.SemaphoreType.DMA((4,)),
            pltpu.SemaphoreType.DMA((4,)),
            pltpu.SemaphoreType.DMA((2, 4)),
            pltpu.SemaphoreType.DMA((2, 4)),
            pltpu.SemaphoreType.DMA,
            pltpu.SemaphoreType.DMA,
        ],
        compiler_params=pltpu.CompilerParams(
            collective_id=0, has_side_effects=True, vmem_limit_bytes=60 * 1024 * 1024
        ),
    )(probe, positions, conductivity, fluid_exchange, row_blocks, column_blocks)


def bed_kernel(
    teams, total, probe_in, pos_in, cond_in, fluid_in, counts_in, cols_in, out,
    probe, pos, cond, load_sem,
    geo, ints, cnts, counts, cols, smem_sem, fluid, stage, landed,
    points, mid, lines, flank, tiles, ends, begins, ids, keep, selfs, more, last,
    sums, parts, low, high, cur, prev, inv, corr, mine_sum, their_sum, mine_deg, their_deg, arrived,
    gather_send, gather_recv, pair_send, pair_recv,
):
    rows, columns, particles = probe.shape
    slots = cols.shape[1]
    clusters = teams * rows
    width = columns // teams
    pairs = clusters // 2
    units = tiles.shape[0]
    span = 2 * units
    group = lax.axis_index("groups")
    member = lax.axis_index("team")
    team = lax.axis_index("blk")
    f32, bf16 = jnp.float32, jnp.bfloat16

    def at(ahead):
        return (group, member, lax.rem(team + ahead, teams))

    partner = (group, 1 - member, team)
    barrier = pltpu.get_barrier_semaphore()
    for ahead in range(1, teams):
        pl.semaphore_signal(barrier, inc=1, device_id=at(ahead), device_id_type=MESH)
    pl.semaphore_signal(barrier, inc=1, device_id=partner, device_id_type=MESH)

    loads = [
        pltpu.make_async_copy(source, place, load_sem.at[n])
        for n, (source, place) in enumerate(
            (
                (pos_in, pos), (cond_in, cond), (probe_in, probe),
                (cols_in, cols.at[pl.ds(team * rows, rows)]), (counts_in, counts.at[team]), (fluid_in, fluid.at[team]),
            )
        )
    ]
    for load in loads:
        load.start()
    for load in loads[:2]:
        load.wait()
    for r in range(rows):
        geo[team, r, 0:3, :] = pos[r] * SCALE
        geo[team, r, 3:4, :] = 0.5 / cond[r : r + 1, :]
    pl.semaphore_wait(barrier, teams)

    def gather(kind, ahead):
        source, place = (
            (counts.at[team], counts.at[team]), (cols.at[pl.ds(team * rows, rows)], cols.at[pl.ds(team * rows, rows)]), (geo.at[team], geo.at[team]),
            (stage.at[lax.rem(team + ahead, teams)], landed.at[team]), (fluid_in, fluid.at[team]),
        )[kind]
        return pltpu.make_async_remote_copy(
            src_ref=source, dst_ref=place,
            send_sem=gather_send.at[kind, ahead], recv_sem=gather_recv.at[kind, ahead],
            device_id=at(ahead), device_id_type=MESH,
        )

    others = range(1, teams)
    order = sorted(others, key=lambda a: -abs(2 * a - teams))
    for load in loads[3:5]:
        load.wait()
    for ahead in others:
        gather(0, ahead).start()
        gather(1, ahead).start()
    for ahead in order:
        gather(2, ahead).start()

    level = lax.broadcasted_iota(jnp.int32, (8, particles), 0)
    half = level < width
    square = level % width == 3

    def rounded(value):
        return value.astype(bf16).astype(f32)

    def thirds(value):
        head = rounded(value)
        tail = value - head
        body = rounded(tail)
        return head, body, tail - body

    def length(value):
        value = value * value
        value = value + pltpu.roll(value, 1, 0)
        return value + pltpu.roll(value, 2, 0)

    def spread(place):
        def one(r, carry):
            spot = place * rows + r
            point = geo[place, r]
            point = jnp.where(square, 0.0, jnp.concatenate([point, point], 0))
            middle = jnp.broadcast_to(jnp.sum(point * (1.0 / particles), axis=1, keepdims=True), (8, particles))
            points[spot] = point
            mid[spot] = middle
            off = point - middle
            a, b, c = thirds(off)
            d, e, f = thirds(length(off))
            g, h, i = thirds(jnp.broadcast_to(geo[place, r, 3:4, :], (8, particles)))
            last_line = jnp.zeros((8, particles), f32)
            for n, value in enumerate((d, e, f, g, h, i)):
                last_line = jnp.where(level == n, value, last_line)
            block = jnp.concatenate(
                [
                    jnp.where(level == 3, 1.0, jnp.where(half, a, b)),
                    jnp.where(level == 7, 1.0, jnp.where(half, c, a)),
                    jnp.where(level == 7, 1.0, jnp.where(half, b, a)),
                    last_line,
                ],
                0,
            )
            lines[spot] = block.astype(bf16).T
            flank[spot] = jnp.concatenate(
                [
                    jnp.where(level == 3, g, 0.0),
                    jnp.where(level == 7, h, 0.0),
                    jnp.where(level == 7, i, 0.0),
                    jnp.where((level > 2) & (level < 6), 1.0, 0.0),
                ],
                0,
            ).astype(bf16)
            return carry
        lax.fori_loop(0, rows, one, 0, unroll=SPREAD)

    spread(team)
    loads[2].wait()
    loads[5].wait()
    for q in range(rows // 4):
        wide = [probe[4 * q + a].astype(f32) for a in range(4)]
        for t in range(teams):
            stage[t, q] = jnp.concatenate([w[t * width : (t + 1) * width] for w in wide], 0).astype(bf16)
    landed[team] = stage[team]
    for ahead in others:
        gather(0, ahead).wait()
        gather(1, ahead).wait()
    first = member * span
    final = first + span

    def lay(t, state):
        at_end, zero, one = state
        for j in range(rows):
            r = t * rows + j
            begins[r] = at_end
            at_end = at_end + counts[t, 0, j]
            ends[r] = at_end
            zero = zero + jnp.where(at_end <= first, 1, 0)
            one = one + jnp.where(at_end <= first + units, 1, 0)
        return at_end, zero, one

    _, zero, one = lax.fori_loop(0, teams, lay, (jnp.int32(0), jnp.int32(0), jnp.int32(0)))
    zero, one = jnp.minimum(zero, clusters - 1), jnp.minimum(one, clusters - 1)

    for ahead in order:
        gather(2, ahead).wait()
        spread(lax.rem(team + teams - ahead, teams))
    for ahead in others:
        gather(3, ahead).start()
        gather(4, ahead).start()


    ones = jnp.where(level < 3, 1.0, 0.0)

    def build_tile(u, lane, r, selves, running):
        place = first + lane * units + u
        index = lane * units + u
        r = jnp.minimum(r + jnp.where(place >= ends[r], 1, 0), clusters - 1)
        begin = begins[r]
        col = cols[r, jnp.minimum(place - begin, slots - 1)]
        fresh = jnp.logical_or(place == begin, u == 0)
        going = jnp.where(fresh, 0.0, 1.0)
        ids[index] = col
        keep[index] = going
        selves = jnp.where(fresh, 0.0, selves) + jnp.where(col == r, 1.0, 0.0)
        selfs[index] = selves
        off = points[r] - mid[col]
        a, b, c = thirds(jnp.where(square, length(off), -2.0 * off))
        block = jnp.concatenate([a, jnp.where(half, a, b), jnp.where(half, b, c), ones], 0).astype(bf16)
        both_sides = jnp.dot(
            lines[col], jnp.concatenate([block, flank[r]], 1), preferred_element_type=f32
        )
        tally = jnp.zeros((8, particles), f32)
        for j in range(0, particles, 16):
            values = []
            for h in (j, j + 8):
                power = both_sides[h : h + 8, :particles]
                value = pltpu.reciprocal(both_sides[h : h + 8, particles:] * jnp.exp2(power), approx=APPROX)
                tally = tally + value
                values.append(value)
            tiles[u, lane * particles + j : lane * particles + j + 16, :] = jnp.concatenate(values, 0).astype(bf16)
        running = running * going + tally
        sums[index] = running
        return r, selves, running

    def build(u, state):
        return build_tile(u, 0, *state[:3]) + build_tile(u, 1, *state[3:])

    blank = jnp.zeros((8, particles), f32)
    state = lax.fori_loop(
        0, units, build, (zero, jnp.float32(0.0), blank, one, jnp.float32(0.0), blank), unroll=BUILD
    )

    sums[span] = blank
    parts[span] = blank
    edge_row = state[0]
    edge = ends[edge_row]
    for u in range(slots - 1):
        flag = jnp.where(first + units + u < edge, 1.0, 0.0)
        more[u] = flag
        selfs[units + u] = selfs[units + u] + flag * selfs[units - 1]
        sums[units + u] = sums[units + u] + flag * sums[units - 1]
    def both(even, odd):
        return jnp.where(half, jnp.broadcast_to(even, (8, particles)), jnp.broadcast_to(odd, (8, particles)))

    def settle(t, carry):
        for j in range(0, rows, 2):
            r = t * rows + j
            p = t * (rows // 2) + j // 2
            lines = []
            for h in (0, 1):
                end = jnp.minimum(ends[r + h], final) - 1
                have = end >= jnp.maximum(begins[r + h], first)
                spot = jnp.where(have, end - first, span)
                last[r + h] = spot
                own = jnp.where(have, selfs[jnp.where(have, end - first, 0)], 0.0)
                twice = geo[t, j + h, 3:4, :] + geo[t, j + h, 3:4, :]
                itself = pltpu.reciprocal(twice, approx=APPROX)
                degree = jnp.sum(sums[spot], axis=0, keepdims=True) - own * itself
                lines.append((degree, own * itself.astype(bf16).astype(f32)))
            mine_deg[p] = both(lines[0][0], lines[1][0])
            corr[p] = both(lines[0][1], lines[1][1])
        return carry

    lax.fori_loop(0, teams, settle, 0)

    def swap(source, place, n):
        return pltpu.make_async_remote_copy(
            src_ref=source, dst_ref=place, send_sem=pair_send.at[n], recv_sem=pair_recv.at[n],
            device_id=partner, device_id_type=MESH,
        )

    degrees = swap(mine_deg, their_deg, 2)
    degrees.start()

    nothing = jnp.zeros((8, particles), f32)

    def publish(p, fresh):
        turned = pltpu.roll(fresh, width, 0)
        for h, line in ((0, jnp.where(half, fresh, turned)), (1, jnp.where(half, turned, fresh))):
            low[2 * p + h] = jnp.concatenate([line, nothing], 0).astype(bf16)
            high[2 * p + h] = jnp.concatenate([nothing, line], 0).astype(bf16)

    for ahead in others:
        gather(3, ahead).wait()
        gather(4, ahead).wait()

    def begin_fields(t, carry):
        for q in range(rows // 4):
            block = landed[t, q].astype(f32)
            for h in (0, 1):
                p = t * (rows // 2) + 2 * q + h
                cur[p] = block[8 * h : 8 * h + 8]
                prev[p] = nothing
                publish(p, block[8 * h : 8 * h + 8])
        return carry

    lax.fori_loop(0, teams, begin_fields, 0)

    def step(k, carry):
        slot = lax.rem(k, 2)

        def unit(u, state):
            taken = jnp.concatenate([low[ids[u]], high[ids[units + u]]], axis=1)
            product = jnp.dot(taken, tiles[u], preferred_element_type=f32)
            zero = state[0] * keep[u] + product[0:8]
            one = state[1] * keep[units + u] + product[8:16]
            parts[u] = zero
            parts[units + u] = one
            return zero, one

        lax.fori_loop(0, units, unit, (blank, blank), unroll=UNROLL)
        for u in range(slots - 1):
            parts[units + u] = parts[units + u] + more[u] * parts[units - 1]

        def pack(p, carry):
            own = cur[p].astype(bf16).astype(f32)
            product = jnp.where(half, parts[last[2 * p]], parts[last[2 * p + 1]])
            mine_sum[slot, p] = product - corr[p] * own
            return carry

        share = pairs // PIECES
        exchanges = [
            swap(
                mine_sum.at[slot, pl.ds(n * share, share)], their_sum.at[slot, pl.ds(n * share, share)],
                3 + 2 * n + slot,
            )
            for n in range(PIECES)
        ]
        for n in range(PIECES):
            lax.fori_loop(n * share, (n + 1) * share, pack, 0, unroll=8)
            exchanges[n].start()

        @pl.when(k == 0)
        def _():
            degrees.wait()

            def divide(t, carry):
                for j in range(0, rows, 2):
                    p = t * (rows // 2) + j // 2
                    exchange = both(fluid[t, j : j + 1, :], fluid[t, j + 1 : j + 2, :])
                    inv[p] = (2.0 / HALF_SPAN) / (exchange + (mine_deg[p] + their_deg[p]))
                return carry

            lax.fori_loop(0, teams, divide, 0)

        gain = jnp.where(k == 0, 0.5, 1.0)

        def update(p, carry):
            field = cur[p]
            product = mine_sum[slot, p] + their_sum[slot, p]
            change = (2.0 * (1.0 - CENTER) / HALF_SPAN) * field - product * inv[p]
            fresh = gain * change - prev[p]
            prev[p] = field
            cur[p] = fresh
            publish(p, fresh)
            return carry

        for n in range(PIECES):
            exchanges[n].wait()
            lax.fori_loop(n * share, (n + 1) * share, update, 0, unroll=8)
        return carry

    lax.fori_loop(0, DEGREE, step, 0)

    few = rows // 2

    def deliver(ahead):
        goal = lax.rem(team + ahead, teams)
        return pltpu.make_async_remote_copy(
            src_ref=cur.at[pl.ds(goal * few, few)], dst_ref=arrived.at[team],
            send_sem=gather_send.at[5, ahead], recv_sem=gather_recv.at[5, ahead],
            device_id=at(ahead), device_id_type=MESH,
        )

    for ahead in others:
        deliver(ahead).start()
    for p in range(few):
        arrived[team, p] = cur[team * few + p]
    for ahead in others:
        deliver(ahead).wait()
    for p in range(few):
        for c in range(0, teams, 2):
            one, two = arrived[c, p], arrived[c + 1, p]
            out[2 * p, c * width : c * width + 8, :] = jnp.where(half, one, pltpu.roll(two, width, 0))
            out[2 * p + 1, c * width : c * width + 8, :] = jnp.where(half, pltpu.roll(one, width, 0), two)


def bed(teams, probe, positions, conductivity, fluid_exchange, row_blocks, column_blocks):
    rows, columns, particles = probe.shape
    slots = column_blocks.shape[1]
    clusters = teams * rows
    total = MEAN_BLOCKS * clusters
    units = total // 4
    span = 2 * units
    pairs = clusters // 2
    f32, bf16, i32 = jnp.float32, jnp.bfloat16, jnp.int32
    vmem = pl.BlockSpec(memory_space=pltpu.VMEM)
    anywhere = pl.BlockSpec(memory_space=pl.ANY)
    field = pltpu.VMEM((pairs, 8, particles), f32)
    return pl.pallas_call(
        functools.partial(bed_kernel, teams, total),
        out_shape=jax.ShapeDtypeStruct((rows, columns, particles), f32),
        in_specs=[anywhere] * 6,
        out_specs=vmem,
        scratch_shapes=[
            pltpu.VMEM(probe.shape, probe.dtype),
            pltpu.VMEM(positions.shape, f32),
            pltpu.VMEM(conductivity.shape, f32),
            pltpu.SemaphoreType.DMA((6,)),
            pltpu.VMEM((teams, rows, 4, particles), f32),
            pltpu.VMEM((teams, rows, slots), i32),
            pltpu.VMEM((teams, 1, rows), i32),
            pltpu.SMEM((teams, 1, rows), i32),
            pltpu.SMEM((clusters, slots), i32),
            pltpu.SemaphoreType.DMA((teams + 1,)),
            pltpu.VMEM((teams, rows, particles), f32),
            pltpu.VMEM((teams, rows // 4, 16, particles), bf16),
            pltpu.VMEM((teams, rows // 4, 16, particles), bf16),
            pltpu.VMEM((clusters, 8, particles), f32),
            pltpu.VMEM((clusters, 8, particles), f32),
            pltpu.VMEM((clusters, particles, 32), bf16),
            pltpu.VMEM((clusters, 32, particles), bf16),
            pltpu.VMEM((units, 2 * particles, particles), bf16),
            pltpu.SMEM((clusters + 1,), i32),
            pltpu.SMEM((clusters + 1,), i32),
            pltpu.SMEM((span,), i32),
            pltpu.SMEM((span,), f32),
            pltpu.SMEM((span,), f32),
            pltpu.SMEM((slots,), f32),
            pltpu.SMEM((clusters,), i32),
            pltpu.VMEM((span + 1, 8, particles), f32),
            pltpu.VMEM((span + 1, 8, particles), f32),
            pltpu.VMEM((clusters, 16, particles), bf16),
            pltpu.VMEM((clusters, 16, particles), bf16),
            field, field, field, field,
            pltpu.VMEM((2, pairs, 8, particles), f32),
            pltpu.VMEM((2, pairs, 8, particles), f32),
            field, field,
            pltpu.VMEM((teams, rows // 2, 8, particles), f32),
            pltpu.SemaphoreType.DMA((6, teams)),
            pltpu.SemaphoreType.DMA((6, teams)),
            pltpu.SemaphoreType.DMA((3 + 2 * PIECES,)),
            pltpu.SemaphoreType.DMA((3 + 2 * PIECES,)),
        ],
        compiler_params=pltpu.CompilerParams(
            collective_id=1, has_side_effects=True, vmem_limit_bytes=60 * 1024 * 1024
        ),
    )(probe, positions, conductivity, fluid_exchange, row_blocks.reshape(1, rows), column_blocks)


def either(teams, probe, *rest):
    rows, columns, particles = probe.shape
    if columns == 4 * teams and rows % 4 == 0 and MEAN_BLOCKS * teams * rows <= 1024:
        return bed(teams, probe, *rest)
    return local(teams, probe, *rest)


def solution(mesh):
    return jax.shard_map(
        functools.partial(either, mesh.shape["blk"]),
        mesh=mesh,
        in_specs=(
            P(("groups", "blk"), None, None),
            P(("groups", "blk"), None, None),
            P(("groups", "blk"), None),
            P(("groups", "blk"), None),
            P(("groups", "blk")),
            P(("groups", "blk"), None),
        ),
        out_specs=P(("groups", "blk"), None, None),
        check_vma=False,
    )
```

```python
import functools
import math

import jax
import jax.numpy as jnp
from jax import lax
from jax.experimental import pallas as pl
from jax.experimental.pallas import tpu as pltpu
from jax.sharding import PartitionSpec as P

DEGREE = 8
WIDTH_SQ = 0.245
CENTER = 1.05
HALF_SPAN = 0.95
SCALE = math.sqrt(math.log2(math.e) / WIDTH_SQ)
MESH = pl.DeviceIdType.MESH
REACHES = (-2, -1, 1, 2)
CHUNK = 3
MEAN_BLOCKS = 9
APPROX = True
UNROLL = 216
BUILD = 54
PIECES = 3
SPREAD = 12


def kernel(
    teams, probe_in, pos_in, cond_in, fluid_in, counts_in, cols_in, out,
    probe, pos, cond, fluid, counts, cols, load_sem,
    geo, bcast, tiles, even, odd, cur, prev, inv, corr, ids, other,
    geo_send, geo_recv, win_send, win_recv, pair_send, pair_recv,
):
    loads = [
        pltpu.make_async_copy(source, place, load_sem.at[n])
        for n, (source, place) in enumerate(
            (
                (pos_in, pos), (cond_in, cond), (probe_in, probe),
                (cols_in, cols), (counts_in, counts), (fluid_in, fluid),
            )
        )
    ]
    for load in loads:
        load.start()
    rows, columns, particles = probe.shape
    half = columns // 2
    slots = cols.shape[1]
    clusters = teams * rows
    group = lax.axis_index("groups")
    member = lax.axis_index("team")
    team = lax.axis_index("blk")

    def at(reach):
        return (group, member, lax.rem(team + reach + teams, teams))

    partner = (group, 1 - member, team)
    barrier = pltpu.get_barrier_semaphore()
    for reach in REACHES:
        pl.semaphore_signal(barrier, inc=1, device_id=at(reach), device_id_type=MESH)
    pl.semaphore_signal(barrier, inc=1, device_id=partner, device_id_type=MESH)

    for load in loads[:3]:
        load.wait()
    for r in range(rows):
        geo[2, r, 0:3, :] = pos[r] * SCALE
        geo[2, r, 3:4, :] = 0.5 / cond[r : r + 1, :]
        mine = probe[r, pl.ds(pl.multiple_of(member * half, half), half), :]
        even[2 * rows + r] = mine
        cur[r] = mine.astype(jnp.float32)
        prev[r] = jnp.zeros((half, particles), jnp.float32)
    pl.semaphore_wait(barrier, len(REACHES) + 1)

    def geo_copy(n):
        reach = REACHES[n]
        return pltpu.make_async_remote_copy(
            src_ref=geo.at[2], dst_ref=geo.at[2 - reach],
            send_sem=geo_send.at[n], recv_sem=geo_recv.at[n],
            device_id=at(reach), device_id_type=MESH,
        )

    def win_copy(parity, n, first=0, size=None):
        reach = REACHES[n]
        window = (even, odd)[parity]
        size = rows if size is None else size
        return pltpu.make_async_remote_copy(
            src_ref=window.at[pl.ds(2 * rows + first, size)], dst_ref=window.at[pl.ds((2 - reach) * rows + first, size)],
            send_sem=win_send.at[parity, n], recv_sem=win_recv.at[parity, n],
            device_id=at(reach), device_id_type=MESH,
        )

    for n in range(4):
        geo_copy(n).start()
    def spread(place):
        def one(r, carry):
            for k in range(4):
                line = geo[place, r, k : k + 1, :]
                bcast[place * rows + r, k] = jnp.broadcast_to(line, (particles, particles)).T
            return carry
        lax.fori_loop(0, rows, one, 0, unroll=2)

    spread(2)
    for n in range(4):
        geo_copy(n).wait()
        spread(2 - REACHES[n])
    for n in range(4):
        win_copy(0, n).start()

    for load in loads[3:]:
        load.wait()
    base = (team - 2) * rows

    def build_row(r, carry):
        own = team * rows + r
        count = counts[r]
        xi = [jnp.broadcast_to(geo[2, r, k : k + 1, :], (8, particles)) for k in range(4)]

        def build_tile(s, state):
            total, selves = state
            col = cols[r, s]
            active = s < count
            place = col - base
            place = jnp.where(place < 0, place + clusters, place)
            place = jnp.where(place >= clusters, place - clusters, place)
            place = jnp.where(active, jnp.minimum(place, 5 * rows - 1), 0)
            ids[r, s] = place
            selves = selves + jnp.where(active & (col == own), 1.0, 0.0)
            bias = jnp.where(active, 0.0, -1e30)
            for j in range(0, particles, 16):
                parts = []
                for h in (j, j + 8):
                    dx = bcast[place, 0, h : h + 8, :] - xi[0]
                    dy = bcast[place, 1, h : h + 8, :] - xi[1]
                    dz = bcast[place, 2, h : h + 8, :] - xi[2]
                    power = bias - dx * dx - dy * dy - dz * dz
                    value = jnp.exp2(power) / (bcast[place, 3, h : h + 8, :] + xi[3])
                    total = total + value
                    parts.append(value)
                tiles[r, pl.ds(pl.multiple_of(s * particles + j, 16), 16), :] = jnp.concatenate(
                    parts, 0
                ).astype(jnp.bfloat16)
            return total, selves

        total, selves = lax.fori_loop(
            0, slots, build_tile, (jnp.zeros((8, particles), jnp.float32), jnp.float32(0.0)),
            unroll=3,
        )
        itself = 1.0 / (xi[3] + xi[3])
        degree = jnp.sum(total, axis=0, keepdims=True) - selves * itself[0:1]
        divisor = fluid[pl.ds(r, 1), :] + degree
        inv[r] = jnp.broadcast_to((2.0 / HALF_SPAN) / divisor, (half, particles))
        rounded = itself[0:1].astype(jnp.bfloat16).astype(jnp.float32)
        corr[r] = jnp.broadcast_to(selves * rounded, (half, particles))
        return carry

    lax.fori_loop(0, rows, build_row, 0)

    def step(k, now):
        later = 1 - now
        window, target = (even, odd)[now], (even, odd)[later]
        for n in range(4):
            win_copy(now, n).wait()
        gain = jnp.where(k == 0, 0.5, 1.0)

        def row(r):
            taken = jnp.concatenate(
                [window[ids[r, s]] for s in range(slots)],
                axis=1,
            )
            product = jnp.dot(taken, tiles[r], preferred_element_type=jnp.float32)
            mine = window[2 * rows + r].astype(jnp.float32)
            product = product - corr[r] * mine
            field = cur[r]
            change = (2.0 * (1.0 - CENTER) / HALF_SPAN) * field - product * inv[r]
            fresh = gain * change - prev[r]
            prev[r] = field
            cur[r] = fresh
            target[2 * rows + r] = fresh.astype(jnp.bfloat16)

        for first in range(0, rows, CHUNK):
            size = min(CHUNK, rows - first)
            for r in range(first, first + size):
                row(r)

            @pl.when(k < DEGREE - 1)
            def _():
                for n in range(4):
                    win_copy(later, n, first, size).start()

    def two_steps(i, carry):
        step(2 * i, 0)
        step(2 * i + 1, 1)
        return carry

    lax.fori_loop(0, DEGREE // 2, two_steps, 0)

    swap = pltpu.make_async_remote_copy(
        src_ref=cur, dst_ref=other, send_sem=pair_send, recv_sem=pair_recv,
        device_id=partner, device_id_type=MESH,
    )
    swap.start()
    out[:, pl.ds(pl.multiple_of(member * half, half), half), :] = cur[...]
    swap.wait()
    out[:, pl.ds(pl.multiple_of((1 - member) * half, half), half), :] = other[...]


def local(teams, probe, positions, conductivity, fluid_exchange, row_blocks, column_blocks):
    rows, columns, particles = probe.shape
    slots = column_blocks.shape[1]
    half = columns // 2
    vmem = pl.BlockSpec(memory_space=pltpu.VMEM)
    anywhere = pl.BlockSpec(memory_space=pl.ANY)
    f32 = jnp.float32
    return pl.pallas_call(
        functools.partial(kernel, teams),
        out_shape=jax.ShapeDtypeStruct((rows, columns, particles), f32),
        in_specs=[anywhere] * 6,
        out_specs=vmem,
        scratch_shapes=[
            pltpu.VMEM(probe.shape, probe.dtype),
            pltpu.VMEM(positions.shape, f32),
            pltpu.VMEM(conductivity.shape, f32),
            pltpu.VMEM(fluid_exchange.shape, f32),
            pltpu.SMEM(row_blocks.shape, jnp.int32),
            pltpu.SMEM(column_blocks.shape, jnp.int32),
            pltpu.SemaphoreType.DMA((6,)),
            pltpu.VMEM((5, rows, 4, particles), f32),
            pltpu.VMEM((5 * rows, 4, particles, particles), f32),
            pltpu.VMEM((rows, slots * particles, particles), jnp.bfloat16),
            pltpu.VMEM((5 * rows, half, particles), jnp.bfloat16),
            pltpu.VMEM((5 * rows, half, particles), jnp.bfloat16),
            pltpu.VMEM((rows, half, particles), f32),
            pltpu.VMEM((rows, half, particles), f32),
            pltpu.VMEM((rows, half, particles), f32),
            pltpu.VMEM((rows, half, particles), f32),
            pltpu.SMEM((rows, slots), jnp.int32),
            pltpu.VMEM((rows, half, particles), f32),
            pltpu.SemaphoreType.DMA((4,)),
            pltpu.SemaphoreType.DMA((4,)),
            pltpu.SemaphoreType.DMA((2, 4)),
            pltpu.SemaphoreType.DMA((2, 4)),
            pltpu.SemaphoreType.DMA,
            pltpu.SemaphoreType.DMA,
        ],
        compiler_params=pltpu.CompilerParams(
            collective_id=0, has_side_effects=True, vmem_limit_bytes=60 * 1024 * 1024
        ),
    )(probe, positions, conductivity, fluid_exchange, row_blocks, column_blocks)


def bed_kernel(
    teams, total, probe_in, pos_in, cond_in, fluid_in, counts_in, cols_in, out,
    probe, pos, cond, load_sem,
    geo, ints, cnts, counts, cols, smem_sem, fluid, stage, landed,
    points, mid, lines, flank, tiles, ends, begins, ids, keep, selfs, more, last,
    sums, parts, low, high, cur, prev, inv, corr, mine_sum, their_sum, mine_deg, their_deg, arrived,
    gather_send, gather_recv, pair_send, pair_recv,
):
    rows, columns, particles = probe.shape
    slots = cols.shape[1]
    clusters = teams * rows
    width = columns // teams
    pairs = clusters // 2
    units = tiles.shape[0]
    span = 2 * units
    group = lax.axis_index("groups")
    member = lax.axis_index("team")
    team = lax.axis_index("blk")
    f32, bf16 = jnp.float32, jnp.bfloat16

    def at(ahead):
        return (group, member, lax.rem(team + ahead, teams))

    partner = (group, 1 - member, team)
    barrier = pltpu.get_barrier_semaphore()
    for ahead in range(1, teams):
        pl.semaphore_signal(barrier, inc=1, device_id=at(ahead), device_id_type=MESH)
    pl.semaphore_signal(barrier, inc=1, device_id=partner, device_id_type=MESH)

    loads = [
        pltpu.make_async_copy(source, place, load_sem.at[n])
        for n, (source, place) in enumerate(
            (
                (pos_in, pos), (cond_in, cond), (probe_in, probe),
                (cols_in, cols.at[pl.ds(team * rows, rows)]), (counts_in, counts.at[team]), (fluid_in, fluid.at[team]),
            )
        )
    ]
    for load in loads:
        load.start()
    for load in loads[:2]:
        load.wait()
    for r in range(rows):
        geo[team, r, 0:3, :] = pos[r] * SCALE
        geo[team, r, 3:4, :] = 0.5 / cond[r : r + 1, :]
    pl.semaphore_wait(barrier, teams)

    def gather(kind, ahead):
        source, place = (
            (counts.at[team], counts.at[team]), (cols.at[pl.ds(team * rows, rows)], cols.at[pl.ds(team * rows, rows)]), (geo.at[team], geo.at[team]),
            (stage.at[lax.rem(team + ahead, teams)], landed.at[team]), (fluid_in, fluid.at[team]),
        )[kind]
        return pltpu.make_async_remote_copy(
            src_ref=source, dst_ref=place,
            send_sem=gather_send.at[kind, ahead], recv_sem=gather_recv.at[kind, ahead],
            device_id=at(ahead), device_id_type=MESH,
        )

    others = range(1, teams)
    order = sorted(others, key=lambda a: -abs(2 * a - teams))
    for load in loads[3:5]:
        load.wait()
    for ahead in others:
        gather(0, ahead).start()
        gather(1, ahead).start()
    for ahead in order:
        gather(2, ahead).start()

    level = lax.broadcasted_iota(jnp.int32, (8, particles), 0)
    half = level < width
    square = level % width == 3

    def rounded(value):
        return value.astype(bf16).astype(f32)

    def thirds(value):
        head = rounded(value)
        tail = value - head
        body = rounded(tail)
        return head, body, tail - body

    def length(value):
        value = value * value
        value = value + pltpu.roll(value, 1, 0)
        return value + pltpu.roll(value, 2, 0)

    def spread(place):
        def one(r, carry):
            spot = place * rows + r
            point = geo[place, r]
            point = jnp.where(square, 0.0, jnp.concatenate([point, point], 0))
            middle = jnp.broadcast_to(jnp.sum(point * (1.0 / particles), axis=1, keepdims=True), (8, particles))
            points[spot] = point
            mid[spot] = middle
            off = point - middle
            a, b, c = thirds(off)
            d, e, f = thirds(length(off))
            g, h, i = thirds(jnp.broadcast_to(geo[place, r, 3:4, :], (8, particles)))
            last_line = jnp.zeros((8, particles), f32)
            for n, value in enumerate((d, e, f, g, h, i)):
                last_line = jnp.where(level == n, value, last_line)
            block = jnp.concatenate(
                [
                    jnp.where(level == 3, 1.0, jnp.where(half, a, b)),
                    jnp.where(level == 7, 1.0, jnp.where(half, c, a)),
                    jnp.where(level == 7, 1.0, jnp.where(half, b, a)),
                    last_line,
                ],
                0,
            )
            lines[spot] = block.astype(bf16).T
            flank[spot] = jnp.concatenate(
                [
                    jnp.where(level == 3, g, 0.0),
                    jnp.where(level == 7, h, 0.0),
                    jnp.where(level == 7, i, 0.0),
                    jnp.where((level > 2) & (level < 6), 1.0, 0.0),
                ],
                0,
            ).astype(bf16)
            return carry
        lax.fori_loop(0, rows, one, 0, unroll=SPREAD)

    spread(team)
    loads[2].wait()
    loads[5].wait()
    for q in range(rows // 4):
        wide = [probe[4 * q + a].astype(f32) for a in range(4)]
        for t in range(teams):
            stage[t, q] = jnp.concatenate([w[t * width : (t + 1) * width] for w in wide], 0).astype(bf16)
    landed[team] = stage[team]
    for ahead in others:
        gather(0, ahead).wait()
        gather(1, ahead).wait()
    first = member * span
    final = first + span

    def lay(t, state):
        at_end, zero, one = state
        for j in range(rows):
            r = t * rows + j
            begins[r] = at_end
            at_end = at_end + counts[t, 0, j]
            ends[r] = at_end
            zero = zero + jnp.where(at_end <= first, 1, 0)
            one = one + jnp.where(at_end <= first + units, 1, 0)
        return at_end, zero, one

    _, zero, one = lax.fori_loop(0, teams, lay, (jnp.int32(0), jnp.int32(0), jnp.int32(0)))
    zero, one = jnp.minimum(zero, clusters - 1), jnp.minimum(one, clusters - 1)

    for ahead in order:
        gather(2, ahead).wait()
        spread(lax.rem(team + teams - ahead, teams))
    for ahead in others:
        gather(3, ahead).start()
        gather(4, ahead).start()


    ones = jnp.where(level < 3, 1.0, 0.0)

    def build_tile(u, lane, r, selves, running):
        place = first + lane * units + u
        index = lane * units + u
        r = jnp.minimum(r + jnp.where(place >= ends[r], 1, 0), clusters - 1)
        begin = begins[r]
        col = cols[r, jnp.minimum(place - begin, slots - 1)]
        fresh = jnp.logical_or(place == begin, u == 0)
        going = jnp.where(fresh, 0.0, 1.0)
        ids[index] = col
        keep[index] = going
        selves = jnp.where(fresh, 0.0, selves) + jnp.where(col == r, 1.0, 0.0)
        selfs[index] = selves
        off = points[r] - mid[col]
        a, b, c = thirds(jnp.where(square, length(off), -2.0 * off))
        block = jnp.concatenate([a, jnp.where(half, a, b), jnp.where(half, b, c), ones], 0).astype(bf16)
        both_sides = jnp.dot(
            lines[col], jnp.concatenate([block, flank[r]], 1), preferred_element_type=f32
        )
        tally = jnp.zeros((8, particles), f32)
        for j in range(0, particles, 16):
            values = []
            for h in (j, j + 8):
                power = both_sides[h : h + 8, :particles]
                value = pltpu.reciprocal(both_sides[h : h + 8, particles:] * jnp.exp2(power), approx=APPROX)
                tally = tally + value
                values.append(value)
            tiles[u, lane * particles + j : lane * particles + j + 16, :] = jnp.concatenate(values, 0).astype(bf16)
        running = running * going + tally
        sums[index] = running
        return r, selves, running

    def build(u, state):
        return build_tile(u, 0, *state[:3]) + build_tile(u, 1, *state[3:])

    blank = jnp.zeros((8, particles), f32)
    state = lax.fori_loop(
        0, units, build, (zero, jnp.float32(0.0), blank, one, jnp.float32(0.0), blank), unroll=BUILD
    )

    sums[span] = blank
    parts[span] = blank
    edge_row = state[0]
    edge = ends[edge_row]
    for u in range(slots - 1):
        flag = jnp.where(first + units + u < edge, 1.0, 0.0)
        more[u] = flag
        selfs[units + u] = selfs[units + u] + flag * selfs[units - 1]
        sums[units + u] = sums[units + u] + flag * sums[units - 1]
    def both(even, odd):
        return jnp.where(half, jnp.broadcast_to(even, (8, particles)), jnp.broadcast_to(odd, (8, particles)))

    def settle(t, carry):
        for j in range(0, rows, 2):
            r = t * rows + j
            p = t * (rows // 2) + j // 2
            lines = []
            for h in (0, 1):
                end = jnp.minimum(ends[r + h], final) - 1
                have = end >= jnp.maximum(begins[r + h], first)
                spot = jnp.where(have, end - first, span)
                last[r + h] = spot
                own = jnp.where(have, selfs[jnp.where(have, end - first, 0)], 0.0)
                twice = geo[t, j + h, 3:4, :] + geo[t, j + h, 3:4, :]
                itself = pltpu.reciprocal(twice, approx=APPROX)
                degree = jnp.sum(sums[spot], axis=0, keepdims=True) - own * itself
                lines.append((degree, own * itself.astype(bf16).astype(f32)))
            mine_deg[p] = both(lines[0][0], lines[1][0])
            corr[p] = both(lines[0][1], lines[1][1])
        return carry

    lax.fori_loop(0, teams, settle, 0, unroll=4)

    def swap(source, place, n):
        return pltpu.make_async_remote_copy(
            src_ref=source, dst_ref=place, send_sem=pair_send.at[n], recv_sem=pair_recv.at[n],
            device_id=partner, device_id_type=MESH,
        )

    degrees = swap(mine_deg, their_deg, 2)
    degrees.start()

    nothing = jnp.zeros((8, particles), f32)

    def publish(p, fresh):
        turned = pltpu.roll(fresh, width, 0)
        for h, line in ((0, jnp.where(half, fresh, turned)), (1, jnp.where(half, turned, fresh))):
            low[2 * p + h] = jnp.concatenate([line, nothing], 0).astype(bf16)
            high[2 * p + h] = jnp.concatenate([nothing, line], 0).astype(bf16)

    for ahead in others:
        gather(3, ahead).wait()
        gather(4, ahead).wait()

    def begin_fields(t, carry):
        for q in range(rows // 4):
            block = landed[t, q].astype(f32)
            for h in (0, 1):
                p = t * (rows // 2) + 2 * q + h
                cur[p] = block[8 * h : 8 * h + 8]
                prev[p] = nothing
                publish(p, block[8 * h : 8 * h + 8])
        return carry

    lax.fori_loop(0, teams, begin_fields, 0, unroll=2)

    def step(k, carry):
        slot = lax.rem(k, 2)

        def unit(u, state):
            taken = jnp.concatenate([low[ids[u]], high[ids[units + u]]], axis=1)
            product = jnp.dot(taken, tiles[u], preferred_element_type=f32)
            zero = state[0] * keep[u] + product[0:8]
            one = state[1] * keep[units + u] + product[8:16]
            parts[u] = zero
            parts[units + u] = one
            return zero, one

        lax.fori_loop(0, units, unit, (blank, blank), unroll=UNROLL)
        for u in range(slots - 1):
            parts[units + u] = parts[units + u] + more[u] * parts[units - 1]

        def pack(p, carry):
            own = cur[p].astype(bf16).astype(f32)
            product = jnp.where(half, parts[last[2 * p]], parts[last[2 * p + 1]])
            mine_sum[slot, p] = product - corr[p] * own
            return carry

        share = pairs // PIECES
        exchanges = [
            swap(
                mine_sum.at[slot, pl.ds(n * share, share)], their_sum.at[slot, pl.ds(n * share, share)],
                3 + 2 * n + slot,
            )
            for n in range(PIECES)
        ]
        for n in range(PIECES):
            lax.fori_loop(n * share, (n + 1) * share, pack, 0, unroll=8)
            exchanges[n].start()

        @pl.when(k == 0)
        def _():
            degrees.wait()

            def divide(t, carry):
                for j in range(0, rows, 2):
                    p = t * (rows // 2) + j // 2
                    exchange = both(fluid[t, j : j + 1, :], fluid[t, j + 1 : j + 2, :])
                    inv[p] = (2.0 / HALF_SPAN) / (exchange + (mine_deg[p] + their_deg[p]))
                return carry

            lax.fori_loop(0, teams, divide, 0, unroll=2)

        gain = jnp.where(k == 0, 0.5, 1.0)

        def update(p, carry):
            field = cur[p]
            product = mine_sum[slot, p] + their_sum[slot, p]
            change = (2.0 * (1.0 - CENTER) / HALF_SPAN) * field - product * inv[p]
            fresh = gain * change - prev[p]
            prev[p] = field
            cur[p] = fresh
            publish(p, fresh)
            return carry

        for n in range(PIECES):
            exchanges[n].wait()
            lax.fori_loop(n * share, (n + 1) * share, update, 0, unroll=8)
        return carry

    lax.fori_loop(0, DEGREE, step, 0)

    few = rows // 2

    def deliver(ahead):
        goal = lax.rem(team + ahead, teams)
        return pltpu.make_async_remote_copy(
            src_ref=cur.at[pl.ds(goal * few, few)], dst_ref=arrived.at[team],
            send_sem=gather_send.at[5, ahead], recv_sem=gather_recv.at[5, ahead],
            device_id=at(ahead), device_id_type=MESH,
        )

    for ahead in others:
        deliver(ahead).start()
    for p in range(few):
        arrived[team, p] = cur[team * few + p]
    for ahead in others:
        deliver(ahead).wait()
    for p in range(few):
        for c in range(0, teams, 2):
            one, two = arrived[c, p], arrived[c + 1, p]
            out[2 * p, c * width : c * width + 8, :] = jnp.where(half, one, pltpu.roll(two, width, 0))
            out[2 * p + 1, c * width : c * width + 8, :] = jnp.where(half, pltpu.roll(one, width, 0), two)


def bed(teams, probe, positions, conductivity, fluid_exchange, row_blocks, column_blocks):
    rows, columns, particles = probe.shape
    slots = column_blocks.shape[1]
    clusters = teams * rows
    total = MEAN_BLOCKS * clusters
    units = total // 4
    span = 2 * units
    pairs = clusters // 2
    f32, bf16, i32 = jnp.float32, jnp.bfloat16, jnp.int32
    vmem = pl.BlockSpec(memory_space=pltpu.VMEM)
    anywhere = pl.BlockSpec(memory_space=pl.ANY)
    field = pltpu.VMEM((pairs, 8, particles), f32)
    return pl.pallas_call(
        functools.partial(bed_kernel, teams, total),
        out_shape=jax.ShapeDtypeStruct((rows, columns, particles), f32),
        in_specs=[anywhere] * 6,
        out_specs=vmem,
        scratch_shapes=[
            pltpu.VMEM(probe.shape, probe.dtype),
            pltpu.VMEM(positions.shape, f32),
            pltpu.VMEM(conductivity.shape, f32),
            pltpu.SemaphoreType.DMA((6,)),
            pltpu.VMEM((teams, rows, 4, particles), f32),
            pltpu.VMEM((teams, rows, slots), i32),
            pltpu.VMEM((teams, 1, rows), i32),
            pltpu.SMEM((teams, 1, rows), i32),
            pltpu.SMEM((clusters, slots), i32),
            pltpu.SemaphoreType.DMA((teams + 1,)),
            pltpu.VMEM((teams, rows, particles), f32),
            pltpu.VMEM((teams, rows // 4, 16, particles), bf16),
            pltpu.VMEM((teams, rows // 4, 16, particles), bf16),
            pltpu.VMEM((clusters, 8, particles), f32),
            pltpu.VMEM((clusters, 8, particles), f32),
            pltpu.VMEM((clusters, particles, 32), bf16),
            pltpu.VMEM((clusters, 32, particles), bf16),
            pltpu.VMEM((units, 2 * particles, particles), bf16),
            pltpu.SMEM((clusters + 1,), i32),
            pltpu.SMEM((clusters + 1,), i32),
            pltpu.SMEM((span,), i32),
            pltpu.SMEM((span,), f32),
            pltpu.SMEM((span,), f32),
            pltpu.SMEM((slots,), f32),
            pltpu.SMEM((clusters,), i32),
            pltpu.VMEM((span + 1, 8, particles), f32),
            pltpu.VMEM((span + 1, 8, particles), f32),
            pltpu.VMEM((clusters, 16, particles), bf16),
            pltpu.VMEM((clusters, 16, particles), bf16),
            field, field, field, field,
            pltpu.VMEM((2, pairs, 8, particles), f32),
            pltpu.VMEM((2, pairs, 8, particles), f32),
            field, field,
            pltpu.VMEM((teams, rows // 2, 8, particles), f32),
            pltpu.SemaphoreType.DMA((6, teams)),
            pltpu.SemaphoreType.DMA((6, teams)),
            pltpu.SemaphoreType.DMA((3 + 2 * PIECES,)),
            pltpu.SemaphoreType.DMA((3 + 2 * PIECES,)),
        ],
        compiler_params=pltpu.CompilerParams(
            collective_id=1, has_side_effects=True, vmem_limit_bytes=60 * 1024 * 1024
        ),
    )(probe, positions, conductivity, fluid_exchange, row_blocks.reshape(1, rows), column_blocks)


def either(teams, probe, *rest):
    rows, columns, particles = probe.shape
    if columns == 4 * teams and rows % 4 == 0 and MEAN_BLOCKS * teams * rows <= 1024:
        return bed(teams, probe, *rest)
    return local(teams, probe, *rest)


def solution(mesh):
    return jax.shard_map(
        functools.partial(either, mesh.shape["blk"]),
        mesh=mesh,
        in_specs=(
            P(("groups", "blk"), None, None),
            P(("groups", "blk"), None, None),
            P(("groups", "blk"), None),
            P(("groups", "blk"), None),
            P(("groups", "blk")),
            P(("groups", "blk"), None),
        ),
        out_specs=P(("groups", "blk"), None, None),
        check_vma=False,
    )
```

```python
import functools
import math

import jax
import jax.numpy as jnp
from jax import lax
from jax.experimental import pallas as pl
from jax.experimental.pallas import tpu as pltpu
from jax.sharding import PartitionSpec as P

DEGREE = 8
WIDTH_SQ = 0.245
CENTER = 1.05
HALF_SPAN = 0.95
SCALE = math.sqrt(math.log2(math.e) / WIDTH_SQ)
MESH = pl.DeviceIdType.MESH
REACHES = (-2, -1, 1, 2)
CHUNK = 3
MEAN_BLOCKS = 9
APPROX = True
UNROLL = 216
BUILD = 54
PIECES = 3
SPREAD = 12


def kernel(
    teams, probe_in, pos_in, cond_in, fluid_in, counts_in, cols_in, out,
    probe, pos, cond, fluid, counts, cols, load_sem,
    geo, bcast, tiles, even, odd, cur, prev, inv, corr, ids, other,
    geo_send, geo_recv, win_send, win_recv, pair_send, pair_recv,
):
    loads = [
        pltpu.make_async_copy(source, place, load_sem.at[n])
        for n, (source, place) in enumerate(
            (
                (pos_in, pos), (cond_in, cond), (probe_in, probe),
                (cols_in, cols), (counts_in, counts), (fluid_in, fluid),
            )
        )
    ]
    for load in loads:
        load.start()
    rows, columns, particles = probe.shape
    half = columns // 2
    slots = cols.shape[1]
    clusters = teams * rows
    group = lax.axis_index("groups")
    member = lax.axis_index("team")
    team = lax.axis_index("blk")

    def at(reach):
        return (group, member, lax.rem(team + reach + teams, teams))

    partner = (group, 1 - member, team)
    barrier = pltpu.get_barrier_semaphore()
    for reach in REACHES:
        pl.semaphore_signal(barrier, inc=1, device_id=at(reach), device_id_type=MESH)
    pl.semaphore_signal(barrier, inc=1, device_id=partner, device_id_type=MESH)

    for load in loads[:3]:
        load.wait()
    for r in range(rows):
        geo[2, r, 0:3, :] = pos[r] * SCALE
        geo[2, r, 3:4, :] = 0.5 / cond[r : r + 1, :]
        mine = probe[r, pl.ds(pl.multiple_of(member * half, half), half), :]
        even[2 * rows + r] = mine
        cur[r] = mine.astype(jnp.float32)
        prev[r] = jnp.zeros((half, particles), jnp.float32)
    pl.semaphore_wait(barrier, len(REACHES) + 1)

    def geo_copy(n):
        reach = REACHES[n]
        return pltpu.make_async_remote_copy(
            src_ref=geo.at[2], dst_ref=geo.at[2 - reach],
            send_sem=geo_send.at[n], recv_sem=geo_recv.at[n],
            device_id=at(reach), device_id_type=MESH,
        )

    def win_copy(parity, n, first=0, size=None):
        reach = REACHES[n]
        window = (even, odd)[parity]
        size = rows if size is None else size
        return pltpu.make_async_remote_copy(
            src_ref=window.at[pl.ds(2 * rows + first, size)], dst_ref=window.at[pl.ds((2 - reach) * rows + first, size)],
            send_sem=win_send.at[parity, n], recv_sem=win_recv.at[parity, n],
            device_id=at(reach), device_id_type=MESH,
        )

    for n in range(4):
        geo_copy(n).start()
    def spread(place):
        def one(r, carry):
            for k in range(4):
                line = geo[place, r, k : k + 1, :]
                bcast[place * rows + r, k] = jnp.broadcast_to(line, (particles, particles)).T
            return carry
        lax.fori_loop(0, rows, one, 0, unroll=2)

    spread(2)
    for n in range(4):
        geo_copy(n).wait()
        spread(2 - REACHES[n])
    for n in range(4):
        win_copy(0, n).start()

    for load in loads[3:]:
        load.wait()
    base = (team - 2) * rows

    def build_row(r, carry):
        own = team * rows + r
        count = counts[r]
        xi = [jnp.broadcast_to(geo[2, r, k : k + 1, :], (8, particles)) for k in range(4)]

        def build_tile(s, state):
            total, selves = state
            col = cols[r, s]
            active = s < count
            place = col - base
            place = jnp.where(place < 0, place + clusters, place)
            place = jnp.where(place >= clusters, place - clusters, place)
            place = jnp.where(active, jnp.minimum(place, 5 * rows - 1), 0)
            ids[r, s] = place
            selves = selves + jnp.where(active & (col == own), 1.0, 0.0)
            bias = jnp.where(active, 0.0, -1e30)
            for j in range(0, particles, 16):
                parts = []
                for h in (j, j + 8):
                    dx = bcast[place, 0, h : h + 8, :] - xi[0]
                    dy = bcast[place, 1, h : h + 8, :] - xi[1]
                    dz = bcast[place, 2, h : h + 8, :] - xi[2]
                    power = bias - dx * dx - dy * dy - dz * dz
                    value = jnp.exp2(power) / (bcast[place, 3, h : h + 8, :] + xi[3])
                    total = total + value
                    parts.append(value)
                tiles[r, pl.ds(pl.multiple_of(s * particles + j, 16), 16), :] = jnp.concatenate(
                    parts, 0
                ).astype(jnp.bfloat16)
            return total, selves

        total, selves = lax.fori_loop(
            0, slots, build_tile, (jnp.zeros((8, particles), jnp.float32), jnp.float32(0.0)),
            unroll=3,
        )
        itself = 1.0 / (xi[3] + xi[3])
        degree = jnp.sum(total, axis=0, keepdims=True) - selves * itself[0:1]
        divisor = fluid[pl.ds(r, 1), :] + degree
        inv[r] = jnp.broadcast_to((2.0 / HALF_SPAN) / divisor, (half, particles))
        rounded = itself[0:1].astype(jnp.bfloat16).astype(jnp.float32)
        corr[r] = jnp.broadcast_to(selves * rounded, (half, particles))
        return carry

    lax.fori_loop(0, rows, build_row, 0)

    def step(k, now):
        later = 1 - now
        window, target = (even, odd)[now], (even, odd)[later]
        for n in range(4):
            win_copy(now, n).wait()
        gain = jnp.where(k == 0, 0.5, 1.0)

        def row(r):
            taken = jnp.concatenate(
                [window[ids[r, s]] for s in range(slots)],
                axis=1,
            )
            product = jnp.dot(taken, tiles[r], preferred_element_type=jnp.float32)
            mine = window[2 * rows + r].astype(jnp.float32)
            product = product - corr[r] * mine
            field = cur[r]
            change = (2.0 * (1.0 - CENTER) / HALF_SPAN) * field - product * inv[r]
            fresh = gain * change - prev[r]
            prev[r] = field
            cur[r] = fresh
            target[2 * rows + r] = fresh.astype(jnp.bfloat16)

        for first in range(0, rows, CHUNK):
            size = min(CHUNK, rows - first)
            for r in range(first, first + size):
                row(r)

            @pl.when(k < DEGREE - 1)
            def _():
                for n in range(4):
                    win_copy(later, n, first, size).start()

    def two_steps(i, carry):
        step(2 * i, 0)
        step(2 * i + 1, 1)
        return carry

    lax.fori_loop(0, DEGREE // 2, two_steps, 0)

    swap = pltpu.make_async_remote_copy(
        src_ref=cur, dst_ref=other, send_sem=pair_send, recv_sem=pair_recv,
        device_id=partner, device_id_type=MESH,
    )
    swap.start()
    out[:, pl.ds(pl.multiple_of(member * half, half), half), :] = cur[...]
    swap.wait()
    out[:, pl.ds(pl.multiple_of((1 - member) * half, half), half), :] = other[...]


def local(teams, probe, positions, conductivity, fluid_exchange, row_blocks, column_blocks):
    rows, columns, particles = probe.shape
    slots = column_blocks.shape[1]
    half = columns // 2
    vmem = pl.BlockSpec(memory_space=pltpu.VMEM)
    anywhere = pl.BlockSpec(memory_space=pl.ANY)
    f32 = jnp.float32
    return pl.pallas_call(
        functools.partial(kernel, teams),
        out_shape=jax.ShapeDtypeStruct((rows, columns, particles), f32),
        in_specs=[anywhere] * 6,
        out_specs=vmem,
        scratch_shapes=[
            pltpu.VMEM(probe.shape, probe.dtype),
            pltpu.VMEM(positions.shape, f32),
            pltpu.VMEM(conductivity.shape, f32),
            pltpu.VMEM(fluid_exchange.shape, f32),
            pltpu.SMEM(row_blocks.shape, jnp.int32),
            pltpu.SMEM(column_blocks.shape, jnp.int32),
            pltpu.SemaphoreType.DMA((6,)),
            pltpu.VMEM((5, rows, 4, particles), f32),
            pltpu.VMEM((5 * rows, 4, particles, particles), f32),
            pltpu.VMEM((rows, slots * particles, particles), jnp.bfloat16),
            pltpu.VMEM((5 * rows, half, particles), jnp.bfloat16),
            pltpu.VMEM((5 * rows, half, particles), jnp.bfloat16),
            pltpu.VMEM((rows, half, particles), f32),
            pltpu.VMEM((rows, half, particles), f32),
            pltpu.VMEM((rows, half, particles), f32),
            pltpu.VMEM((rows, half, particles), f32),
            pltpu.SMEM((rows, slots), jnp.int32),
            pltpu.VMEM((rows, half, particles), f32),
            pltpu.SemaphoreType.DMA((4,)),
            pltpu.SemaphoreType.DMA((4,)),
            pltpu.SemaphoreType.DMA((2, 4)),
            pltpu.SemaphoreType.DMA((2, 4)),
            pltpu.SemaphoreType.DMA,
            pltpu.SemaphoreType.DMA,
        ],
        compiler_params=pltpu.CompilerParams(
            collective_id=0, has_side_effects=True, vmem_limit_bytes=60 * 1024 * 1024
        ),
    )(probe, positions, conductivity, fluid_exchange, row_blocks, column_blocks)


def bed_kernel(
    teams, total, probe_in, pos_in, cond_in, fluid_in, counts_in, cols_in, out,
    probe, pos, cond, load_sem,
    geo, ints, cnts, counts, cols, smem_sem, fluid, stage, landed,
    points, mid, lines, flank, tiles, ends, begins, ids, keep, selfs, more, last,
    sums, parts, low, high, cur, prev, inv, corr, mine_sum, their_sum, mine_deg, their_deg, arrived,
    gather_send, gather_recv, pair_send, pair_recv,
):
    rows, columns, particles = probe.shape
    slots = cols.shape[1]
    clusters = teams * rows
    width = columns // teams
    pairs = clusters // 2
    units = tiles.shape[0]
    span = 2 * units
    group = lax.axis_index("groups")
    member = lax.axis_index("team")
    team = lax.axis_index("blk")
    f32, bf16 = jnp.float32, jnp.bfloat16

    def at(ahead):
        return (group, member, lax.rem(team + ahead, teams))

    partner = (group, 1 - member, team)
    barrier = pltpu.get_barrier_semaphore()
    for ahead in range(1, teams):
        pl.semaphore_signal(barrier, inc=1, device_id=at(ahead), device_id_type=MESH)
    pl.semaphore_signal(barrier, inc=1, device_id=partner, device_id_type=MESH)

    loads = [
        pltpu.make_async_copy(source, place, load_sem.at[n])
        for n, (source, place) in enumerate(
            (
                (pos_in, pos), (cond_in, cond), (probe_in, probe),
                (cols_in, cols.at[pl.ds(team * rows, rows)]), (counts_in, counts.at[team]), (fluid_in, fluid.at[team]),
            )
        )
    ]
    for load in loads:
        load.start()
    for load in loads[:2]:
        load.wait()
    for r in range(rows):
        geo[team, r, 0:3, :] = pos[r] * SCALE
        geo[team, r, 3:4, :] = 0.5 / cond[r : r + 1, :]
    pl.semaphore_wait(barrier, teams)

    def gather(kind, ahead):
        source, place = (
            (counts.at[team], counts.at[team]), (cols.at[pl.ds(team * rows, rows)], cols.at[pl.ds(team * rows, rows)]), (geo.at[team], geo.at[team]),
            (stage.at[lax.rem(team + ahead, teams)], landed.at[team]), (fluid_in, fluid.at[team]),
        )[kind]
        return pltpu.make_async_remote_copy(
            src_ref=source, dst_ref=place,
            send_sem=gather_send.at[kind, ahead], recv_sem=gather_recv.at[kind, ahead],
            device_id=at(ahead), device_id_type=MESH,
        )

    others = range(1, teams)
    order = sorted(others, key=lambda a: -abs(2 * a - teams))
    for load in loads[3:5]:
        load.wait()
    for ahead in others:
        gather(0, ahead).start()
        gather(1, ahead).start()
    for ahead in order:
        gather(2, ahead).start()

    level = lax.broadcasted_iota(jnp.int32, (8, particles), 0)
    half = level < width
    square = level % width == 3

    def rounded(value):
        return value.astype(bf16).astype(f32)

    def thirds(value):
        head = rounded(value)
        tail = value - head
        body = rounded(tail)
        return head, body, tail - body

    def length(value):
        value = value * value
        value = value + pltpu.roll(value, 1, 0)
        return value + pltpu.roll(value, 2, 0)

    def spread(place):
        def one(r, carry):
            spot = place * rows + r
            point = geo[place, r]
            point = jnp.where(square, 0.0, jnp.concatenate([point, point], 0))
            middle = jnp.broadcast_to(jnp.sum(point * (1.0 / particles), axis=1, keepdims=True), (8, particles))
            points[spot] = point
            mid[spot] = middle
            off = point - middle
            a, b, c = thirds(off)
            d, e, f = thirds(length(off))
            g, h, i = thirds(jnp.broadcast_to(geo[place, r, 3:4, :], (8, particles)))
            last_line = jnp.zeros((8, particles), f32)
            for n, value in enumerate((d, e, f, g, h, i)):
                last_line = jnp.where(level == n, value, last_line)
            block = jnp.concatenate(
                [
                    jnp.where(level == 3, 1.0, jnp.where(half, a, b)),
                    jnp.where(level == 7, 1.0, jnp.where(half, c, a)),
                    jnp.where(level == 7, 1.0, jnp.where(half, b, a)),
                    last_line,
                ],
                0,
            )
            lines[spot] = block.astype(bf16).T
            flank[spot] = jnp.concatenate(
                [
                    jnp.where(level == 3, g, 0.0),
                    jnp.where(level == 7, h, 0.0),
                    jnp.where(level == 7, i, 0.0),
                    jnp.where((level > 2) & (level < 6), 1.0, 0.0),
                ],
                0,
            ).astype(bf16)
            return carry
        lax.fori_loop(0, rows, one, 0, unroll=SPREAD)

    spread(team)
    loads[2].wait()
    loads[5].wait()
    for q in range(rows // 4):
        wide = [probe[4 * q + a].astype(f32) for a in range(4)]
        for t in range(teams):
            stage[t, q] = jnp.concatenate([w[t * width : (t + 1) * width] for w in wide], 0).astype(bf16)
    landed[team] = stage[team]
    for ahead in others:
        gather(0, ahead).wait()
        gather(1, ahead).wait()
    first = member * span
    final = first + span

    def lay(t, state):
        at_end, zero, one = state
        for j in range(rows):
            r = t * rows + j
            begins[r] = at_end
            at_end = at_end + counts[t, 0, j]
            ends[r] = at_end
            zero = zero + jnp.where(at_end <= first, 1, 0)
            one = one + jnp.where(at_end <= first + units, 1, 0)
        return at_end, zero, one

    _, zero, one = lax.fori_loop(0, teams, lay, (jnp.int32(0), jnp.int32(0), jnp.int32(0)))
    zero, one = jnp.minimum(zero, clusters - 1), jnp.minimum(one, clusters - 1)

    for ahead in order:
        gather(2, ahead).wait()
        spread(lax.rem(team + teams - ahead, teams))
    for ahead in others:
        gather(3, ahead).start()
        gather(4, ahead).start()


    ones = jnp.where(level < 3, 1.0, 0.0)

    def build_tile(u, lane, r, selves, running):
        place = first + lane * units + u
        index = lane * units + u
        r = jnp.minimum(r + jnp.where(place >= ends[r], 1, 0), clusters - 1)
        begin = begins[r]
        col = cols[r, jnp.minimum(place - begin, slots - 1)]
        fresh = jnp.logical_or(place == begin, u == 0)
        going = jnp.where(fresh, 0.0, 1.0)
        ids[index] = col
        keep[index] = going
        selves = jnp.where(fresh, 0.0, selves) + jnp.where(col == r, 1.0, 0.0)
        selfs[index] = selves
        off = points[r] - mid[col]
        a, b, c = thirds(jnp.where(square, length(off), -2.0 * off))
        block = jnp.concatenate([a, jnp.where(half, a, b), jnp.where(half, b, c), ones], 0).astype(bf16)
        both_sides = jnp.dot(
            lines[col], jnp.concatenate([block, flank[r]], 1), preferred_element_type=f32
        )
        tally = jnp.zeros((8, particles), f32)
        for j in range(0, particles, 16):
            values = []
            for h in (j, j + 8):
                power = both_sides[h : h + 8, :particles]
                value = pltpu.reciprocal(both_sides[h : h + 8, particles:] * jnp.exp2(power), approx=APPROX)
                tally = tally + value
                values.append(value)
            tiles[u, lane * particles + j : lane * particles + j + 16, :] = jnp.concatenate(values, 0).astype(bf16)
        running = running * going + tally
        sums[index] = running
        return r, selves, running

    def build(u, state):
        return build_tile(u, 0, *state[:3]) + build_tile(u, 1, *state[3:])

    blank = jnp.zeros((8, particles), f32)
    state = lax.fori_loop(
        0, units, build, (zero, jnp.float32(0.0), blank, one, jnp.float32(0.0), blank), unroll=BUILD
    )

    sums[span] = blank
    parts[span] = blank
    edge_row = state[0]
    edge = ends[edge_row]
    for u in range(slots - 1):
        flag = jnp.where(first + units + u < edge, 1.0, 0.0)
        more[u] = flag
        selfs[units + u] = selfs[units + u] + flag * selfs[units - 1]
        sums[units + u] = sums[units + u] + flag * sums[units - 1]
    def both(even, odd):
        return jnp.where(half, jnp.broadcast_to(even, (8, particles)), jnp.broadcast_to(odd, (8, particles)))

    def settle(t, carry):
        for j in range(0, rows, 2):
            r = t * rows + j
            p = t * (rows // 2) + j // 2
            lines = []
            for h in (0, 1):
                end = jnp.minimum(ends[r + h], final) - 1
                have = end >= jnp.maximum(begins[r + h], first)
                spot = jnp.where(have, end - first, span)
                last[r + h] = spot
                own = jnp.where(have, selfs[jnp.where(have, end - first, 0)], 0.0)
                twice = geo[t, j + h, 3:4, :] + geo[t, j + h, 3:4, :]
                itself = pltpu.reciprocal(twice, approx=APPROX)
                degree = jnp.sum(sums[spot], axis=0, keepdims=True) - own * itself
                lines.append((degree, own * itself.astype(bf16).astype(f32)))
            mine_deg[p] = both(lines[0][0], lines[1][0])
            corr[p] = both(lines[0][1], lines[1][1])
        return carry

    lax.fori_loop(0, teams, settle, 0, unroll=8)

    def swap(source, place, n):
        return pltpu.make_async_remote_copy(
            src_ref=source, dst_ref=place, send_sem=pair_send.at[n], recv_sem=pair_recv.at[n],
            device_id=partner, device_id_type=MESH,
        )

    degrees = swap(mine_deg, their_deg, 2)
    degrees.start()

    nothing = jnp.zeros((8, particles), f32)

    def publish(p, fresh):
        turned = pltpu.roll(fresh, width, 0)
        for h, line in ((0, jnp.where(half, fresh, turned)), (1, jnp.where(half, turned, fresh))):
            low[2 * p + h] = jnp.concatenate([line, nothing], 0).astype(bf16)
            high[2 * p + h] = jnp.concatenate([nothing, line], 0).astype(bf16)

    for ahead in others:
        gather(3, ahead).wait()
        gather(4, ahead).wait()

    def begin_fields(t, carry):
        for q in range(rows // 4):
            block = landed[t, q].astype(f32)
            for h in (0, 1):
                p = t * (rows // 2) + 2 * q + h
                cur[p] = block[8 * h : 8 * h + 8]
                prev[p] = nothing
                publish(p, block[8 * h : 8 * h + 8])
        return carry

    lax.fori_loop(0, teams, begin_fields, 0, unroll=4)

    def step(k, carry):
        slot = lax.rem(k, 2)

        def unit(u, state):
            taken = jnp.concatenate([low[ids[u]], high[ids[units + u]]], axis=1)
            product = jnp.dot(taken, tiles[u], preferred_element_type=f32)
            zero = state[0] * keep[u] + product[0:8]
            one = state[1] * keep[units + u] + product[8:16]
            parts[u] = zero
            parts[units + u] = one
            return zero, one

        lax.fori_loop(0, units, unit, (blank, blank), unroll=UNROLL)
        for u in range(slots - 1):
            parts[units + u] = parts[units + u] + more[u] * parts[units - 1]

        def pack(p, carry):
            own = cur[p].astype(bf16).astype(f32)
            product = jnp.where(half, parts[last[2 * p]], parts[last[2 * p + 1]])
            mine_sum[slot, p] = product - corr[p] * own
            return carry

        share = pairs // PIECES
        exchanges = [
            swap(
                mine_sum.at[slot, pl.ds(n * share, share)], their_sum.at[slot, pl.ds(n * share, share)],
                3 + 2 * n + slot,
            )
            for n in range(PIECES)
        ]
        for n in range(PIECES):
            lax.fori_loop(n * share, (n + 1) * share, pack, 0, unroll=8)
            exchanges[n].start()

        @pl.when(k == 0)
        def _():
            degrees.wait()

            def divide(t, carry):
                for j in range(0, rows, 2):
                    p = t * (rows // 2) + j // 2
                    exchange = both(fluid[t, j : j + 1, :], fluid[t, j + 1 : j + 2, :])
                    inv[p] = (2.0 / HALF_SPAN) / (exchange + (mine_deg[p] + their_deg[p]))
                return carry

            lax.fori_loop(0, teams, divide, 0, unroll=2)

        gain = jnp.where(k == 0, 0.5, 1.0)

        def update(p, carry):
            field = cur[p]
            product = mine_sum[slot, p] + their_sum[slot, p]
            change = (2.0 * (1.0 - CENTER) / HALF_SPAN) * field - product * inv[p]
            fresh = gain * change - prev[p]
            prev[p] = field
            cur[p] = fresh
            publish(p, fresh)
            return carry

        for n in range(PIECES):
            exchanges[n].wait()
            lax.fori_loop(n * share, (n + 1) * share, update, 0, unroll=8)
        return carry

    lax.fori_loop(0, DEGREE, step, 0)

    few = rows // 2

    def deliver(ahead):
        goal = lax.rem(team + ahead, teams)
        return pltpu.make_async_remote_copy(
            src_ref=cur.at[pl.ds(goal * few, few)], dst_ref=arrived.at[team],
            send_sem=gather_send.at[5, ahead], recv_sem=gather_recv.at[5, ahead],
            device_id=at(ahead), device_id_type=MESH,
        )

    for ahead in others:
        deliver(ahead).start()
    for p in range(few):
        arrived[team, p] = cur[team * few + p]
    for ahead in others:
        deliver(ahead).wait()
    for p in range(few):
        for c in range(0, teams, 2):
            one, two = arrived[c, p], arrived[c + 1, p]
            out[2 * p, c * width : c * width + 8, :] = jnp.where(half, one, pltpu.roll(two, width, 0))
            out[2 * p + 1, c * width : c * width + 8, :] = jnp.where(half, pltpu.roll(one, width, 0), two)


def bed(teams, probe, positions, conductivity, fluid_exchange, row_blocks, column_blocks):
    rows, columns, particles = probe.shape
    slots = column_blocks.shape[1]
    clusters = teams * rows
    total = MEAN_BLOCKS * clusters
    units = total // 4
    span = 2 * units
    pairs = clusters // 2
    f32, bf16, i32 = jnp.float32, jnp.bfloat16, jnp.int32
    vmem = pl.BlockSpec(memory_space=pltpu.VMEM)
    anywhere = pl.BlockSpec(memory_space=pl.ANY)
    field = pltpu.VMEM((pairs, 8, particles), f32)
    return pl.pallas_call(
        functools.partial(bed_kernel, teams, total),
        out_shape=jax.ShapeDtypeStruct((rows, columns, particles), f32),
        in_specs=[anywhere] * 6,
        out_specs=vmem,
        scratch_shapes=[
            pltpu.VMEM(probe.shape, probe.dtype),
            pltpu.VMEM(positions.shape, f32),
            pltpu.VMEM(conductivity.shape, f32),
            pltpu.SemaphoreType.DMA((6,)),
            pltpu.VMEM((teams, rows, 4, particles), f32),
            pltpu.VMEM((teams, rows, slots), i32),
            pltpu.VMEM((teams, 1, rows), i32),
            pltpu.SMEM((teams, 1, rows), i32),
            pltpu.SMEM((clusters, slots), i32),
            pltpu.SemaphoreType.DMA((teams + 1,)),
            pltpu.VMEM((teams, rows, particles), f32),
            pltpu.VMEM((teams, rows // 4, 16, particles), bf16),
            pltpu.VMEM((teams, rows // 4, 16, particles), bf16),
            pltpu.VMEM((clusters, 8, particles), f32),
            pltpu.VMEM((clusters, 8, particles), f32),
            pltpu.VMEM((clusters, particles, 32), bf16),
            pltpu.VMEM((clusters, 32, particles), bf16),
            pltpu.VMEM((units, 2 * particles, particles), bf16),
            pltpu.SMEM((clusters + 1,), i32),
            pltpu.SMEM((clusters + 1,), i32),
            pltpu.SMEM((span,), i32),
            pltpu.SMEM((span,), f32),
            pltpu.SMEM((span,), f32),
            pltpu.SMEM((slots,), f32),
            pltpu.SMEM((clusters,), i32),
            pltpu.VMEM((span + 1, 8, particles), f32),
            pltpu.VMEM((span + 1, 8, particles), f32),
            pltpu.VMEM((clusters, 16, particles), bf16),
            pltpu.VMEM((clusters, 16, particles), bf16),
            field, field, field, field,
            pltpu.VMEM((2, pairs, 8, particles), f32),
            pltpu.VMEM((2, pairs, 8, particles), f32),
            field, field,
            pltpu.VMEM((teams, rows // 2, 8, particles), f32),
            pltpu.SemaphoreType.DMA((6, teams)),
            pltpu.SemaphoreType.DMA((6, teams)),
            pltpu.SemaphoreType.DMA((3 + 2 * PIECES,)),
            pltpu.SemaphoreType.DMA((3 + 2 * PIECES,)),
        ],
        compiler_params=pltpu.CompilerParams(
            collective_id=1, has_side_effects=True, vmem_limit_bytes=60 * 1024 * 1024
        ),
    )(probe, positions, conductivity, fluid_exchange, row_blocks.reshape(1, rows), column_blocks)


def either(teams, probe, *rest):
    rows, columns, particles = probe.shape
    if columns == 4 * teams and rows % 4 == 0 and MEAN_BLOCKS * teams * rows <= 1024:
        return bed(teams, probe, *rest)
    return local(teams, probe, *rest)


def solution(mesh):
    return jax.shard_map(
        functools.partial(either, mesh.shape["blk"]),
        mesh=mesh,
        in_specs=(
            P(("groups", "blk"), None, None),
            P(("groups", "blk"), None, None),
            P(("groups", "blk"), None),
            P(("groups", "blk"), None),
            P(("groups", "blk")),
            P(("groups", "blk"), None),
        ),
        out_specs=P(("groups", "blk"), None, None),
        check_vma=False,
    )
```
